128 devices in a mesh: rep: 8 (over z, y_hi), expert: 16 (over y_lo, x, core).
Axes of the slice: x: 4, y: 4 (y_hi: 2, y_lo: 2; y = y_hi * 2 + y_lo), z: 4, core: 2. Of those that a mesh axis runs over, the one named last changes fastest.
Arguments:
- tokens: bfloat16 [16384, 2048], P(('rep', 'expert')), may hold values from -6 to 6
- norm_gain: float32 [2048], replicated, may hold values from 0.1 to 1.9
- router: bfloat16 [2048, 128], P('rep'), may hold values from -0.125 to 0.125
- routes: int32 [16384, 8], P(('rep', 'expert')), may hold values from 0 to 127, all different within a row; in each aligned block of 128 rows (0 to 127, 128 to 255, ...) at most 12 rows name the same one
- placement: int32 [128], replicated, may hold values from 0 to 127, each once
- w_gate: bfloat16 [128, 2048, 768], P(('rep', 'expert')), may hold values from -0.125 to 0.125
- w_up: bfloat16 [128, 2048, 768], P(('rep', 'expert')), may hold values from -0.125 to 0.125
- w_down: bfloat16 [128, 768, 2048], P(('rep', 'expert')), may hold values from -0.21875 to 0.21875
Outputs:
- moe_out: bfloat16 [16384, 2048], P(('rep', 'expert'))
The draws below stay inside these ranges and needn't reach their ends.
Inputs may be any that keep to these rules, and one draw needn't show every extreme that they name: `routes`: each token's 8 experts differ. Among the 128 tokens of one device at most 12 rows name any one expert, and in some devices' rows one expert is named exactly 12 times. `placement`: A permutation. Weight slot s lies on the device numbered s over rep then expert.
All inputs are finite; a program needn't handle non-finite values.
Results may differ from the reference program's by a relative error of at most 0.0075.
Values may be sent and summed in bfloat16 or wider, within the bound.
A program may use at most 128 MiB of HBM per device.

```python
import math
import jax
import jax.numpy as jnp
import numpy as np
from jax import lax

D = 2048
FF = 768
TOP = 8
TOK_DEV = 128
EXPERTS = 128
TOKENS = 16384
CAP = 12
N_REP = 8
N_EXPERT = 16


def levels(rng, shape, pieces, low, top_value):
    level, own = 1.0, jax.random.fold_in(rng, 6)
    for axis_at, parts in pieces:
        steps = jnp.exp(jax.random.uniform(jax.random.fold_in(own, axis_at), (parts,), jnp.float32, low / len(pieces), top_value / len(pieces)))
        level = level * jnp.repeat(steps, shape[axis_at] // parts).reshape([-1 if axis == axis_at else 1 for axis in range(len(shape))])
    return level


def routed_block(rng, own, number, rows, amount, top, reach, slope):
    ranking = jax.random.permutation(rng, amount)
    packed, ordinary = portions_of(amount, rows * top, reach, slope, True), portions_of(amount, rows * top, reach, slope, False)
    places = jnp.arange(amount)

    def named(sizes, rotation):
        used = int((sizes > 0).sum())
        fixed = max(1, used // 4)
        passed = fixed + (places - fixed + rotation * (used - fixed)) % max(1, amount - fixed)
        return jnp.zeros((amount,), jnp.int32).at[ranking[jnp.where(places < fixed, places, passed)]].set(jnp.asarray(sizes, jnp.int32))

    sizes = jnp.where(number % 4 == 0, named(packed, number // 4), named(ordinary, number - number // 4 - 1))
    mixed = jax.random.permutation(jax.random.fold_in(own, 3), amount)
    source_of, taker = mixed[0:amount // 2 * 2:2], mixed[1:amount // 2 * 2:2]
    slack = jnp.minimum(sizes[source_of] - 1, reach - sizes[taker]) // 2
    slack = jnp.where((source_of == ranking[0]) | (taker == ranking[0]) | (sizes[taker] == 0), 0, jnp.maximum(slack, 0))
    passed = jax.random.randint(jax.random.fold_in(own, 4), (amount // 2,), 0, 1 << 20) % (slack + 1)
    sizes = sizes.at[source_of].add(-passed).at[taker].add(passed)
    items = jnp.searchsorted(jnp.cumsum(sizes), jnp.arange(rows * top), side="right").astype(jnp.int32)
    grid = items.reshape(top, rows).T
    grid = grid[jax.random.permutation(jax.random.fold_in(own, 1), rows)]
    rotation = jax.random.randint(jax.random.fold_in(own, 2), (rows, 1), 0, top)
    return jnp.take_along_axis(grid, (jnp.arange(top)[None, :] + rotation) % top, axis=1)


def portions_of(amount, total, most, lean, full):
    portions = [(1 << 20) // math.isqrt(standing ** lean) + 1 for standing in range(1, amount + 1)]
    largest = most if full else min(most, max(-(-total // amount), total * portions[0] // sum(portions)))
    least = 1 if total - largest >= amount - 1 else 0
    counts, rest = [largest] + [least] * (amount - 1), total - largest - least * (amount - 1)
    while rest > 0:
        candidates = [i for i in range(1, amount) if counts[i] < largest] or [i for i in range(1, amount) if counts[i] < most]
        mass, left = sum([portions[i] for i in candidates]), rest
        for i in candidates:
            more = min(most - counts[i], max(1, left * portions[i] // mass), rest)
            counts[i] = counts[i] + more
            rest = rest - more
    return np.array(counts)


def bell_draw(rng, shape, deviation, reach, split=(), held_as=jnp.bfloat16):
    values = deviation * jax.random.normal(rng, shape, jnp.float32)
    if split:
        values = values * levels(rng, shape, split, -0.22, 0.18)
    return jnp.clip(values, -reach, reach).astype(held_as)


def setup_inputs(seed: int = 0) -> dict:
    key_list = jax.random.split(jax.random.key(seed), 9)
    tokens = bell_draw(key_list[0], (TOKENS, D), 1.0, 6.0, ((0, 128),))
    norm_gain = jnp.clip(1.0 + 0.18 * jax.random.normal(key_list[1], (D,), jnp.float32), 0.1, 1.9)
    router = bell_draw(key_list[2], (D, EXPERTS), D ** -0.5, 0.125, ((0, 8),))
    routes_keys = jax.random.split(jax.random.fold_in(key_list[3], 1), TOKENS // TOK_DEV)
    routes_turns = jax.random.permutation(jax.random.fold_in(key_list[3], 3), TOKENS // TOK_DEV)
    routes = jax.vmap(lambda own, number: routed_block(jax.random.fold_in(key_list[3], 2), own, number, TOK_DEV, EXPERTS, TOP, CAP, 2))(routes_keys, routes_turns).reshape((TOKENS, TOP))
    placement = jax.random.permutation(key_list[4], EXPERTS).astype(jnp.int32)
    w_gate = bell_draw(key_list[5], (EXPERTS, D, FF), D ** -0.5, 0.125, ((0, 128),))
    w_up = bell_draw(key_list[6], (EXPERTS, D, FF), D ** -0.5, 0.125, ((0, 128),))
    w_down = bell_draw(key_list[7], (EXPERTS, FF, D), FF ** -0.5, 0.21875, ((0, 128),))
    return dict(tokens=tokens, norm_gain=norm_gain, router=router, routes=routes, placement=placement, w_gate=w_gate, w_up=w_up, w_down=w_down)


def reference(tokens, norm_gain, router, routes, placement, w_gate, w_up, w_down):
    values = tokens.astype(jnp.float32)
    scale = lax.rsqrt(lax.optimization_barrier(jnp.mean(values * values, axis=-1, keepdims=True)) + 1e-06)
    normed = (values * scale * norm_gain[None, :]).astype(jnp.bfloat16)
    logits = jnp.dot(normed, router, preferred_element_type=jnp.float32)
    picked = jnp.take_along_axis(logits, routes, axis=1)
    powers = jnp.exp(picked)
    shares = (powers / lax.optimization_barrier(jnp.sum(powers, axis=1, keepdims=True))).reshape(-1)
    flat_routes = routes.reshape(-1)
    bound = N_REP * N_EXPERT * CAP

    def one_expert(accumulated, expert_id):
        chosen = flat_routes == expert_id
        members = jnp.nonzero(chosen, size=bound, fill_value=0)[0].astype(jnp.int32)
        live_mask = (jnp.arange(bound, dtype=jnp.int32) < jnp.sum(chosen.astype(jnp.int32))).astype(jnp.float32)
        slot_index = placement[expert_id]
        token_index = members // TOP
        selected = normed[token_index]
        gate_proj = jnp.dot(selected, w_gate[slot_index], preferred_element_type=jnp.float32)
        up_proj = jnp.dot(selected, w_up[slot_index], preferred_element_type=jnp.float32)
        hidden = (jax.nn.silu(gate_proj) * up_proj).astype(jnp.bfloat16)
        output_row = jnp.dot(hidden, w_down[slot_index], preferred_element_type=jnp.float32).astype(jnp.bfloat16)
        output_row = lax.optimization_barrier(output_row).astype(jnp.float32)
        weighted = output_row * (shares[members] * live_mask)[:, None]
        return (accumulated.at[token_index].add(weighted), None)
    start = jnp.zeros((TOKENS, D), jnp.float32)
    total_sum, unused = lax.scan(one_expert, start, jnp.arange(EXPERTS, dtype=jnp.int32))
    return total_sum.astype(jnp.bfloat16)
```

```python
import jax
import jax.numpy as jnp
from jax import lax
from jax.experimental import pallas as pl
from jax.experimental.pallas import tpu as pltpu
from jax.sharding import PartitionSpec as P

MESH = pl.DeviceIdType.MESH
TOK = 128
WIDTH = 2048
HIDDEN = 768
SIDE = 4
ROUNDS = 3
SLOTS = 4
DEVICES = 128
GROUPS = (
    (0, 768, (0, 1, 2)),
    (768, 640, (1, 2, 0)),
    (1408, 640, (2, 0, 1)),
)
NT = (((1,), (1,)), ((), ()))


def iota(shape, dim):
    return lax.broadcasted_iota(jnp.int32, shape, dim)


def dot(a, b):
    return jnp.dot(a, b, preferred_element_type=jnp.float32)


def dot_nt(a, b):
    return lax.dot_general(a, b, NT, preferred_element_type=jnp.float32)


def kernel(
    tokens, gain, router, routes, placement, w_gate, w_up, w_down, out,
    blocks, ranks, weights, packed, hop2, arrived, back3, back2, back1, total,
    gate_v, up_v, down_v, normed, table, stacked, hidden, slot_of, rank_x, share_x,
    w_sem, t_send, t_recv, s1_send, s1_recv, q_send, q_recv, p_send, p_recv,
    s2_send, s2_recv, s3_send, s3_recv, r3_send, r3_recv, r2_send, r2_recv, r1_send, r1_recv,
):
    rep = lax.axis_index("rep")
    exp = lax.axis_index("expert")
    core = exp % 2
    at = (rep // 2, (rep % 2) * 2 + exp // 8, (exp // 2) % 4)

    def device(pos, c):
        z, y, x = pos
        return (z * 2 + y // 2, (y % 2) * 8 + x * 2 + c)

    def along(axis, value, c):
        pos = list(at)
        pos[axis] = value
        return device(pos, c)

    def near(axis, step):
        return (at[axis] + step) % SIDE

    def remote(src, dst, send, recv, dev):
        return pltpu.make_async_remote_copy(
            src_ref=src, dst_ref=dst, send_sem=send, recv_sem=recv,
            device_id=dev, device_id_type=MESH,
        )

    loads = [
        pltpu.make_async_copy(w_gate.at[0], gate_v, w_sem.at[0]),
        pltpu.make_async_copy(w_up.at[0], up_v, w_sem.at[1]),
        pltpu.make_async_copy(w_down.at[0], down_v, w_sem.at[2]),
    ]
    for load in loads:
        load.start()

    barrier = pltpu.get_barrier_semaphore()
    greeted = [along(a, near(a, i), (core + d) % 2) for a in range(3) for i in (1, 2, 3) for d in (0, 1)]
    greeted.append(device(at, 1 - core))
    greeted += [device((near(0, i), near(1, 2), at[2]), core) for i in (1, 2, 3)]
    for dev in greeted:
        pl.semaphore_signal(barrier, inc=1, device_id=dev, device_id_type=MESH)

    values = tokens[...].astype(jnp.float32)
    scale = lax.rsqrt(jnp.mean(values * values, axis=-1, keepdims=True) + 1e-06)
    normed[...] = (values * scale * gain[...]).astype(jnp.bfloat16)
    for g, (first, width, axes) in enumerate(GROUPS):
        blocks[g][pl.ds(pl.multiple_of(at[axes[0]] * TOK, TOK), TOK), :] = normed[:, first:first + width]

    member = jnp.zeros((TOK, DEVICES), jnp.float32)
    lanes = iota((TOK, DEVICES), 1)
    for k in range(8):
        member = member + jnp.where(routes[:, k:k + 1] == lanes, 1.0, 0.0)
    holder = jnp.where(placement[...] == iota((DEVICES, DEVICES), 0), 1.0, 0.0).astype(jnp.bfloat16)
    by_slot = dot_nt(member.astype(jnp.bfloat16), holder)
    before = jnp.where(iota((TOK, TOK), 1) < iota((TOK, TOK), 0), 1.0, 0.0).astype(jnp.bfloat16)
    rank = jnp.where(by_slot > 0.5, dot(before, by_slot.astype(jnp.bfloat16)), -1.0).astype(jnp.bfloat16)
    for g, (first, width, axes) in enumerate(GROUPS):
        ranks[g, pl.ds(pl.multiple_of(at[axes[0]] * TOK, TOK), TOK), :] = rank
    table[pl.ds(pl.multiple_of(rep * 256, 256), 256), :] = router[...]

    pl.semaphore_wait(barrier, len(greeted))

    def own(g, where=None):
        position = at[GROUPS[g][2][0]] if where is None else where
        return pl.ds(pl.multiple_of(position * TOK, TOK), TOK)

    def s1(g, i, where=None):
        a = GROUPS[g][2][0]
        return remote(blocks[g].at[own(g)], blocks[g].at[own(g, where)], s1_send.at[g, i], s1_recv.at[g, i],
                      along(a, near(a, i), core))

    def sq(g, i, where=None):
        a = GROUPS[g][2][0]
        return remote(ranks.at[g, own(g)], ranks.at[g, own(g, where)], q_send.at[g, i], q_recv.at[g, i],
                      along(a, near(a, i), core))

    def sp(g, i, where=None):
        a = GROUPS[g][2][0]
        return remote(weights.at[g, own(g)], weights.at[g, own(g, where)], p_send.at[g, i], p_recv.at[g, i],
                      along(a, near(a, i), core))

    def shard(r):
        return table.at[pl.ds(pl.multiple_of(r * 256, 256), 256)]

    def st(i, r=None):
        return remote(shard(rep), shard(rep if r is None else r), t_send.at[i], t_recv.at[i], ((rep + i) % 8, exp))

    for g in range(3):
        for i in (2, 1, 3):
            sq(g, i).start()
    for i in (2, 1, 3):
        for g in range(3):
            s1(g, i).start()
    for i in range(1, 8):
        st(i).start()

    row = iota((TOK, SIDE * TOK), 0)
    col = iota((TOK, SIDE * TOK), 1)
    slot_of[...] = jnp.where((row // 4) % 4 == col // TOK, row % 4, 1000).astype(jnp.float32)

    def chosen(g, v):
        a1, a2, a3 = GROUPS[g][2]
        r = iota((TOK, DEVICES), 0)
        s = iota((TOK, DEVICES), 1)
        pos = [None, None, None]
        pos[a1] = at[a1]
        pos[a2] = v
        pos[a3] = r // 32
        wanted = pos[0] * 32 + pos[1] * 8 + pos[2] * 2 + (r // 16) % 2
        return jnp.where(s == wanted, 1.0, 0.0).astype(jnp.bfloat16)

    def swap(g):
        r = iota((256, 256), 0)
        c = iota((256, 256), 1)
        a, b, d, s = r // 64, (r // 16) % 4, (r // 4) % 4, r % 4
        if g == 0:
            wanted = d * 64 + b * 16 + a * 4 + s
        else:
            wanted = a * 64 + d * 16 + b * 4 + s
        return jnp.where(c == wanted, 1.0, 0.0).astype(jnp.bfloat16)

    def s2(g, q, i, where=None):
        a = GROUPS[g][2][1]
        v = near(a, i)
        return remote(packed[g].at[q, pl.ds(v * 8, 8)], hop2[g].at[q, at[a] if where is None else where],
                      s2_send.at[g, q, i], s2_recv.at[g, q, i], along(a, v, core))

    def s3(g, q, i, d, where=None):
        a = GROUPS[g][2][2]
        u, c = near(a, i), (core + d) % 2
        src = hop2[g].at[q, :, u * 2 + c]
        dst = arrived[g].at[q, core * 4 + at[a] if where is None else where]
        if i == 0 and d == 0:
            return pltpu.make_async_copy(src, dst, s3_recv.at[g, q, 0])
        return remote(src, dst, s3_send.at[g, q, i * 2 + d], s3_recv.at[g, q, i * 2 + d], along(a, u, c))

    def r3(g, q, i, d, where=None):
        a = GROUPS[g][2][2]
        u, c = near(a, i), (core + d) % 2
        src = packed[g].at[q, pl.ds((c * 4 + u) * 4, 4)]
        dst = back3[g].at[q, :, at[a] * 2 + core if where is None else where]
        if i == 0 and d == 0:
            return pltpu.make_async_copy(src, dst, r3_recv.at[g, q, 0])
        return remote(src, dst, r3_send.at[g, q, i * 2 + d], r3_recv.at[g, q, i * 2 + d], along(a, u, c))

    def r2(g, q, i, where=None):
        a = GROUPS[g][2][1]
        v = near(a, i)
        src, dst = back3[g].at[q, v], back2[g].at[q, at[a] if where is None else where]
        if i == 0:
            return pltpu.make_async_copy(src, dst, r2_recv.at[g, q, 0])
        return remote(src, dst, r2_send.at[g, q, i], r2_recv.at[g, q, i], along(a, v, core))

    def r1(g, i):
        a = GROUPS[g][2][0]
        return remote(blocks[g].at[own(g, near(a, i))], back1[g].at[i - 1], r1_send.at[g, i], r1_recv.at[g, i],
                      along(a, near(a, i), core))

    PAIRS = [(i, d) for i in (2, 1, 3, 0) for d in (0, 1)]

    def gather(q):
        slot = slot_of[...] + (q * SLOTS).astype(jnp.float32)
        for i in (2, 1, 3, 0):
            for g, (first, width, axes) in enumerate(GROUPS):
                v = near(axes[1], i)
                found = dot_nt(chosen(g, v), ranks[g])
                pick = jnp.where(found == slot, 1.0, 0.0).astype(jnp.bfloat16)
                rows = dot(pick, blocks[g][...]).astype(jnp.bfloat16).reshape(8, 16, width)
                if i == 0:
                    hop2[g][q, v] = rows
                else:
                    packed[g][q, pl.ds(v * 8, 8)] = rows
                    s2(g, q, i).start()

    def forward(q):
        for g in range(3):
            for i in (1, 2, 3):
                s2(g, q, i, near(GROUPS[g][2][1], -i)).wait_recv()
            for i, d in PAIRS:
                s3(g, q, i, d).start()

    def expert(q):
        for g, (first, width, axes) in enumerate(GROUPS):
            for i, d in PAIRS:
                copy = s3(g, q, i, d, ((core + d) % 2) * 4 + near(axes[2], -i))
                if i == 0 and d == 0:
                    copy.wait()
                else:
                    copy.wait_recv()
            for c in (0, 1):
                part = arrived[g][q, pl.ds(c * 4, 4)]
                if g == 2:
                    for y in range(4):
                        for z in range(4):
                            at_row = c * 256 + z * 64 + y * 16
                            stacked[at_row:at_row + 16, first:first + width] = part[y, z]
                else:
                    stacked[c * 256:(c + 1) * 256, first:first + width] = dot(
                        swap(g), part.reshape(256, width)).astype(jnp.bfloat16)

        def tile(n, carry):
            cols = pl.ds(pl.multiple_of(n * 256, 256), 256)
            gate = dot(stacked[...], gate_v[:, cols])
            up = dot(stacked[...], up_v[:, cols])
            hidden[:, cols] = (gate / (1.0 + jnp.exp(-gate)) * up).astype(jnp.bfloat16)
            return carry

        lax.fori_loop(0, HIDDEN // 256, tile, 0)
        for g, (first, width, axes) in enumerate(GROUPS):
            result = dot(hidden[...], down_v[:, first:first + width]).astype(jnp.bfloat16)
            for i in (1, 2, 3):
                s2(g, q, i).wait_send()
            for c in (0, 1):
                half = result[c * 256:(c + 1) * 256]
                if g == 2:
                    half = half.reshape(4, 4, 16, width)
                    for y in range(4):
                        for z in range(4):
                            packed[g][q, c * 16 + y * 4 + z] = half[z, y]
                else:
                    packed[g][q, pl.ds(c * 16, 16)] = dot(swap(g), half).astype(jnp.bfloat16).reshape(16, 16, width)
            for i, d in PAIRS:
                r3(g, q, i, d).start()

    def back(q):
        for g, (first, width, axes) in enumerate(GROUPS):
            for i, d in PAIRS:
                copy = r3(g, q, i, d, near(axes[2], -i) * 2 + (core + d) % 2)
                if i == 0 and d == 0:
                    copy.wait()
                else:
                    copy.wait_recv()
            for i in (2, 1, 3, 0):
                r2(g, q, i).start()

    def combine(q):
        for g, (first, width, axes) in enumerate(GROUPS):
            for i in (1, 2, 3):
                r2(g, q, i, near(axes[1], -i)).wait_recv()
            r2(g, q, 0).wait()
            slot = (q * SLOTS).astype(jnp.float32)
            r = iota((SIDE * TOK, SIDE * TOK), 0)
            s = iota((SIDE * TOK, SIDE * TOK), 1)
            wanted = jnp.where((s // 4) % 4 == r // TOK, s % 4, 1000).astype(jnp.float32) + slot
            mix = jnp.where(rank_x[g].astype(jnp.float32) == wanted, share_x[g].astype(jnp.float32), 0.0)
            total[g][...] += dot(mix.astype(jnp.bfloat16), back2[g][q].reshape(SIDE * TOK, width))

            @pl.when(q == ROUNDS - 1)
            def _():
                for i in (1, 2, 3):
                    s1(g, i).wait_send()
                blocks[g][...] = total[g][...].astype(jnp.bfloat16)
                for i in (2, 1, 3):
                    r1(g, i).start()

    def shares():
        for i in range(1, 8):
            st(i, (rep + 8 - i) % 8).wait_recv()
        logits = dot(normed[...], table[...])
        member = jnp.zeros((TOK, DEVICES), jnp.float32)
        lanes = iota((TOK, DEVICES), 1)
        for k in range(8):
            member = member + jnp.where(routes[:, k:k + 1] == lanes, 1.0, 0.0)
        powers = jnp.where(member > 0.5, jnp.exp(logits), 0.0)
        share = (powers / jnp.sum(powers, axis=1, keepdims=True)).astype(jnp.bfloat16)
        holder = jnp.where(placement[...] == iota((DEVICES, DEVICES), 0), 1.0, 0.0).astype(jnp.bfloat16)
        share = dot_nt(share, holder).astype(jnp.bfloat16)
        for g in range(3):
            weights[g, own(g), :] = share
        for g in range(3):
            for i in (2, 1, 3):
                sp(g, i).start()

    def expand():
        for g, (first, width, axes) in enumerate(GROUPS):
            for i in (1, 2, 3):
                sp(g, i, near(axes[0], -i)).wait_recv()
            total[g][...] = jnp.zeros(total[g].shape, jnp.float32)
            for v in range(SIDE):
                pick = chosen(g, v)
                rank_x[g, :, v * TOK:(v + 1) * TOK] = dot_nt(ranks[g], pick).astype(jnp.bfloat16)
                share_x[g, :, v * TOK:(v + 1) * TOK] = dot_nt(weights[g], pick).astype(jnp.bfloat16)

    for g, (first, width, axes) in enumerate(GROUPS):
        for i in (1, 2, 3):
            sq(g, i, near(axes[0], -i)).wait_recv()
            s1(g, i, near(axes[0], -i)).wait_recv()

    def step(k, carry):
        def stage(lag, run):
            @pl.when(jnp.logical_and(k >= lag, k < lag + ROUNDS))
            def _():
                run(k - lag)

        def once(when, run):
            @pl.when(k == when)
            def _():
                run()

        stage(0, gather)
        once(1, shares)
        stage(1, forward)
        once(2, expand)

        @pl.when(k == 2)
        def _():
            for load in loads:
                load.wait()

        stage(2, expert)
        stage(3, back)
        stage(4, combine)
        return carry

    lax.fori_loop(0, ROUNDS + 4, step, 0)

    for g, (first, width, axes) in enumerate(GROUPS):
        result = total[g][own(g), :]
        for i in (1, 2, 3):
            r1(g, i).wait_recv()
            result = result + back1[g][i - 1].astype(jnp.float32)
        out[:, first:first + width] = result.astype(jnp.bfloat16)

    for i in range(1, 8):
        st(i).wait_send()
    for g in range(3):
        for i in (1, 2, 3):
            sq(g, i).wait_send()
            sp(g, i).wait_send()
            r1(g, i).wait_send()

    def drain(q, carry):
        for g in range(3):
            for i, d in PAIRS:
                if i or d:
                    s3(g, q, i, d).wait_send()
                    r3(g, q, i, d).wait_send()
            for i in (1, 2, 3):
                r2(g, q, i).wait_send()
        return carry

    lax.fori_loop(0, ROUNDS, drain, 0)


def per_group(shape):
    return [pltpu.VMEM(shape(width), jnp.bfloat16) for _, width, _ in GROUPS]


def flat_kernel(*refs):
    args, rest = refs[:9], list(refs[9:])

    def take(n):
        head = rest[:n]
        del rest[:n]
        return head

    blocks = take(3)
    ranks, weights = take(2)
    packed, hop2, arrived, back3, back2, back1, total = (take(3) for _ in range(7))
    kernel(*args, blocks, ranks, weights, packed, hop2, arrived, back3, back2, back1, total, *rest)


def per_device(tokens, norm_gain, router, routes, placement, w_gate, w_up, w_down):
    dma = pltpu.SemaphoreType.DMA
    bf = jnp.bfloat16
    scratch = (
        per_group(lambda w: (SIDE * TOK, w))
        + [pltpu.VMEM((3, SIDE * TOK, DEVICES), bf), pltpu.VMEM((3, SIDE * TOK, DEVICES), bf)]
        + per_group(lambda w: (ROUNDS, 32, 16, w))
        + per_group(lambda w: (ROUNDS, 4, 8, 16, w))
        + per_group(lambda w: (ROUNDS, 8, 4, 16, w))
        + per_group(lambda w: (ROUNDS, 4, 8, 16, w))
        + per_group(lambda w: (ROUNDS, 4, 8, 16, w))
        + per_group(lambda w: (3, TOK, w))
        + [pltpu.VMEM((SIDE * TOK, w), jnp.float32) for _, w, _ in GROUPS]
        + [
            pltpu.VMEM((WIDTH, HIDDEN), bf),
            pltpu.VMEM((WIDTH, HIDDEN), bf),
            pltpu.VMEM((HIDDEN, WIDTH), bf),
            pltpu.VMEM((TOK, WIDTH), bf),
            pltpu.VMEM((WIDTH, DEVICES), bf),
            pltpu.VMEM((SIDE * TOK, WIDTH), bf),
            pltpu.VMEM((SIDE * TOK, HIDDEN), bf),
            pltpu.VMEM((TOK, SIDE * TOK), jnp.float32),
            pltpu.VMEM((3, SIDE * TOK, SIDE * TOK), bf),
            pltpu.VMEM((3, SIDE * TOK, SIDE * TOK), bf),
            dma((3,)),
            dma((8,)), dma((8,)),
            dma((3, 4)), dma((3, 4)),
            dma((3, 4)), dma((3, 4)),
            dma((3, 4)), dma((3, 4)),
            dma((3, ROUNDS, 4)), dma((3, ROUNDS, 4)),
            dma((3, ROUNDS, 8)), dma((3, ROUNDS, 8)),
            dma((3, ROUNDS, 8)), dma((3, ROUNDS, 8)),
            dma((3, ROUNDS, 4)), dma((3, ROUNDS, 4)),
            dma((3, 4)), dma((3, 4)),
        ]
    )
    vmem = pl.BlockSpec(memory_space=pltpu.VMEM)
    whole = pl.BlockSpec(memory_space=pl.ANY)
    return pl.pallas_call(
        flat_kernel,
        name="moe",
        out_shape=jax.ShapeDtypeStruct((TOK, WIDTH), bf),
        in_specs=[vmem] * 5 + [whole] * 3,
        out_specs=vmem,
        scratch_shapes=scratch,
        compiler_params=pltpu.CompilerParams(
            collective_id=0, has_side_effects=True, vmem_limit_bytes=63 * 2**20
        ),
        cost_estimate=pl.CostEstimate(flops=15 * 10**9, bytes_accessed=11 * 10**6, transcendentals=10**6),
    )(tokens, norm_gain.reshape(1, WIDTH), router, routes, placement.reshape(1, DEVICES), w_gate, w_up, w_down)


def solution(mesh):
    placed = (
        P(("rep", "expert"), None),
        P(),
        P("rep", None),
        P(("rep", "expert"), None),
        P(),
        P(("rep", "expert"), None, None),
        P(("rep", "expert"), None, None),
        P(("rep", "expert"), None, None),
    )
    return jax.shard_map(
        per_device,
        mesh=mesh,
        in_specs=placed,
        out_specs=P(("rep", "expert"), None),
        check_vma=False,
    )
```

```python
import jax
import jax.numpy as jnp
from jax import lax
from jax.experimental import pallas as pl
from jax.experimental.pallas import tpu as pltpu
from jax.sharding import PartitionSpec as P

MESH = pl.DeviceIdType.MESH
TOK = 128
WIDTH = 2048
HIDDEN = 768
SIDE = 4
ROUNDS = 3
SLOTS = 4
DEVICES = 128
GROUPS = (
    (0, 768, (2, 0, 1)),
    (768, 640, (0, 1, 2)),
    (1408, 640, (1, 2, 0)),
)
NT = (((1,), (1,)), ((), ()))
TN = (((0,), (0,)), ((), ()))
PIECE = 32


def iota(shape, dim):
    return lax.broadcasted_iota(jnp.int32, shape, dim)


def dot(a, b):
    return jnp.dot(a, b, preferred_element_type=jnp.float32)


def dot_nt(a, b):
    return lax.dot_general(a, b, NT, preferred_element_type=jnp.float32)


def dot_tn(a, b):
    return lax.dot_general(a, b, TN, preferred_element_type=jnp.float32)


def kernel(
    tokens, gain, router, routes, placement, w_gate, w_up, w_down, out,
    blocks, ranks, weights, packed, hop2, arrived, back3, back2, back1, total,
    gate_v, up_v, down_v, normed, table, pieces, stacked, hidden, slot_of, mix,
    tokens_v, gain_v, routes_v, placement_v, ranks_out, shares_out,
    w_sem, in_sem, out_sem, t_send, t_recv, u_send, u_recv,
    s1_send, s1_recv, q_send, q_recv, p_send, p_recv, s2_send, s2_recv, s3_send, s3_recv, r3_send, r3_recv, r2_send, r2_recv, r1_send, r1_recv,
):
    rep = lax.axis_index("rep")
    exp = lax.axis_index("expert")
    core = exp % 2
    at = (rep // 2, (rep % 2) * 2 + exp // 8, (exp // 2) % 4)

    def device(pos, c):
        z, y, x = pos
        return (z * 2 + y // 2, (y % 2) * 8 + x * 2 + c)

    def along(axis, value, c):
        pos = list(at)
        pos[axis] = value
        return device(pos, c)

    def near(axis, step):
        return (at[axis] + step) % SIDE

    def remote(src, dst, send, recv, dev):
        return pltpu.make_async_remote_copy(
            src_ref=src, dst_ref=dst, send_sem=send, recv_sem=recv,
            device_id=dev, device_id_type=MESH,
        )

    barrier = pltpu.get_barrier_semaphore()
    greeted = [along(a, near(a, i), (core + d) % 2) for a in range(3) for i in (1, 2, 3) for d in (0, 1)]
    greeted.append(device(at, 1 - core))
    greeted += [device((near(0, i), near(1, 2), at[2]), core) for i in (1, 2, 3)]
    for dev in greeted:
        pl.semaphore_signal(barrier, inc=1, device_id=dev, device_id_type=MESH)

    mine = core * 4 + at[2]
    operands = [
        pltpu.make_async_copy(tokens, tokens_v, in_sem.at[0]),
        pltpu.make_async_copy(gain, gain_v, in_sem.at[1]),
        pltpu.make_async_copy(routes, routes_v, in_sem.at[2]),
        pltpu.make_async_copy(placement, placement_v, in_sem.at[3]),
        pltpu.make_async_copy(
            router.at[pl.ds(pl.multiple_of(mine * PIECE, PIECE), PIECE)], pieces.at[mine, rep], in_sem.at[4]),
    ]
    for load in operands:
        load.start()
    loads = [
        pltpu.make_async_copy(w_gate.at[0], gate_v, w_sem.at[0]),
        pltpu.make_async_copy(w_up.at[0], up_v, w_sem.at[1]),
        pltpu.make_async_copy(w_down.at[0], down_v, w_sem.at[2]),
    ]
    for load in loads:
        load.start()

    operands[0].wait()
    operands[1].wait()
    values = tokens_v[...].astype(jnp.float32)
    scale = lax.rsqrt(jnp.mean(values * values, axis=-1, keepdims=True) + 1e-06)
    normed[...] = (values * scale * gain_v[...]).astype(jnp.bfloat16)
    for g, (first, width, axes) in enumerate(GROUPS):
        blocks[g][pl.ds(pl.multiple_of(at[axes[0]] * TOK, TOK), TOK), :] = normed[:, first:first + width]

    def holder(g):
        a1, a2, a3 = GROUPS[g][2]
        r = iota((DEVICES, DEVICES), 0)
        pos = [None, None, None]
        pos[a1] = r // 32
        pos[a2] = (r // 8) % 4
        pos[a3] = (r // 2) % 4
        wanted = pos[0] * 32 + pos[1] * 8 + pos[2] * 2 + r % 2
        return jnp.where(placement_v[...] == wanted, 1.0, 0.0).astype(jnp.bfloat16)

    def members():
        found = jnp.zeros((DEVICES, TOK), jnp.float32)
        rows = iota((DEVICES, TOK), 0)
        for k in range(8):
            found = found + jnp.where(routes_v[k:k + 1, :] == rows, 1.0, 0.0)
        return found

    operands[2].wait()
    operands[3].wait()
    member = members()
    before = jnp.where(iota((TOK, TOK), 0) < iota((TOK, TOK), 1), 1.0, 0.0).astype(jnp.bfloat16)
    rank = jnp.where(member > 0.5, dot(member.astype(jnp.bfloat16), before), -1.0).astype(jnp.bfloat16)
    for g, (first, width, axes) in enumerate(GROUPS):
        ranks_out[g] = dot(holder(g), rank).astype(jnp.bfloat16)
        ranks[g, :, pl.ds(pl.multiple_of(at[axes[0]] * TOK, TOK), TOK)] = ranks_out[
            g, pl.ds(pl.multiple_of(at[axes[0]] * 32, 32), 32), :]
    operands[4].wait()

    pl.semaphore_wait(barrier, len(greeted))

    def own(g, where=None):
        position = at[GROUPS[g][2][0]] if where is None else where
        return pl.ds(pl.multiple_of(position * TOK, TOK), TOK)

    def s1(g, i, where=None):
        a = GROUPS[g][2][0]
        return remote(blocks[g].at[own(g)], blocks[g].at[own(g, where)], s1_send.at[g, i], s1_recv.at[g, i],
                      along(a, near(a, i), core))

    def lane(g, where=None):
        position = at[GROUPS[g][2][0]] if where is None else where
        return pl.ds(pl.multiple_of(position * TOK, TOK), TOK)

    def sq(g, i, where=None):
        a = GROUPS[g][2][0]
        v = near(a, i)
        return remote(ranks_out.at[g, pl.ds(pl.multiple_of(v * 32, 32), 32)], ranks.at[g, :, lane(g, where)],
                      q_send.at[g, i], q_recv.at[g, i], along(a, v, core))

    def sp(g, i, where=None):
        a = GROUPS[g][2][0]
        v = near(a, i)
        return remote(shares_out.at[g, pl.ds(pl.multiple_of(v * 32, 32), 32)], weights.at[g, :, lane(g, where)],
                      p_send.at[g, i], p_recv.at[g, i], along(a, v, core))

    def st(i, r=None):
        return remote(pieces.at[mine, rep], pieces.at[mine, rep if r is None else r],
                      t_send.at[i], t_recv.at[i], ((rep + i) % 8, exp))

    def su(i, where=None):
        return remote(pieces.at[mine], pieces.at[mine if where is None else core * 4 + where],
                      u_send.at[i], u_recv.at[i], along(2, near(2, i), core))

    def sv(c=None):
        here = core if c is None else c
        return remote(pieces.at[pl.ds(core * 4, 4)], pieces.at[pl.ds(here * 4, 4)],
                      u_send.at[0], u_recv.at[0], device(at, 1 - core))

    for i in (2, 1, 3):
        for g in range(3):
            s1(g, i).start()
    for g in range(3):
        for i in (2, 1, 3):
            sq(g, i).start()
    for i in range(1, 8):
        st(i).start()

    row = iota((TOK, SIDE * TOK), 0)
    col = iota((TOK, SIDE * TOK), 1)
    slot_of[...] = jnp.where((row // 4) % 4 == col // TOK, row % 4, 1000).astype(jnp.float32)

    def spread(v, plane):
        r = iota((TOK, 32), 0)
        pick = jnp.where(iota((TOK, 32), 1) == v * 8 + r // 16, 1.0, 0.0).astype(jnp.bfloat16)
        return dot(pick, plane)

    def swap(g):
        r = iota((256, 256), 0)
        c = iota((256, 256), 1)
        a, b, d, s = r // 64, (r // 16) % 4, (r // 4) % 4, r % 4
        if GROUPS[g][2][0] == 0:
            wanted = d * 64 + b * 16 + a * 4 + s
        else:
            wanted = a * 64 + d * 16 + b * 4 + s
        return jnp.where(c == wanted, 1.0, 0.0).astype(jnp.bfloat16)

    def s2(g, q, i, where=None):
        a = GROUPS[g][2][1]
        v = near(a, i)
        return remote(packed[g].at[q, pl.ds(v * 8, 8)], hop2[g].at[q, at[a] if where is None else where],
                      s2_send.at[g, q, i], s2_recv.at[g, q, i], along(a, v, core))

    def s3(g, q, i, d, where=None):
        a = GROUPS[g][2][2]
        u, c = near(a, i), (core + d) % 2
        src = hop2[g].at[q, :, u * 2 + c]
        dst = arrived[g].at[q, core * 4 + at[a] if where is None else where]
        if i == 0 and d == 0:
            return pltpu.make_async_copy(src, dst, s3_recv.at[g, q, 0])
        return remote(src, dst, s3_send.at[g, q, i * 2 + d], s3_recv.at[g, q, i * 2 + d], along(a, u, c))

    def r3(g, q, i, d, where=None):
        a = GROUPS[g][2][2]
        u, c = near(a, i), (core + d) % 2
        src = packed[g].at[q, pl.ds((c * 4 + u) * 4, 4)]
        dst = back3[g].at[q, :, at[a] * 2 + core if where is None else where]
        if i == 0 and d == 0:
            return pltpu.make_async_copy(src, dst, r3_recv.at[g, q, 0])
        return remote(src, dst, r3_send.at[g, q, i * 2 + d], r3_recv.at[g, q, i * 2 + d], along(a, u, c))

    def r2(g, q, i, where=None):
        a = GROUPS[g][2][1]
        v = near(a, i)
        src, dst = back3[g].at[q, v], back2[g].at[q, at[a] if where is None else where]
        if i == 0:
            return pltpu.make_async_copy(src, dst, r2_recv.at[g, q, 0])
        return remote(src, dst, r2_send.at[g, q, i], r2_recv.at[g, q, i], along(a, v, core))

    def r1(g, i):
        a = GROUPS[g][2][0]
        return remote(blocks[g].at[own(g, near(a, i))], back1[g].at[i - 1], r1_send.at[g, i], r1_recv.at[g, i],
                      along(a, near(a, i), core))

    PAIRS = [(i, d) for i in (2, 1, 3, 0) for d in (0, 1)]

    def gather(q):
        slot = slot_of[...] + (q * SLOTS).astype(jnp.float32)
        for i in (2, 1, 3, 0):
            for g, (first, width, axes) in enumerate(GROUPS):
                v = near(axes[1], i)
                found = spread(v, ranks[g])
                pick = jnp.where(found == slot, 1.0, 0.0).astype(jnp.bfloat16)
                rows = dot(pick, blocks[g][...]).astype(jnp.bfloat16).reshape(8, 16, width)
                if i == 0:
                    hop2[g][q, v] = rows
                else:
                    packed[g][q, pl.ds(v * 8, 8)] = rows
                    s2(g, q, i).start()

    def forward(q):
        for g in range(3):
            for i in (1, 2, 3):
                s2(g, q, i, near(GROUPS[g][2][1], -i)).wait_recv()
            for i, d in PAIRS:
                s3(g, q, i, d).start()

    def expert(q):
        for g, (first, width, axes) in enumerate(GROUPS):
            for i, d in PAIRS:
                copy = s3(g, q, i, d, ((core + d) % 2) * 4 + near(axes[2], -i))
                if i == 0 and d == 0:
                    copy.wait()
                else:
                    copy.wait_recv()
            for c in (0, 1):
                part = arrived[g][q, pl.ds(c * 4, 4)]
                if axes[0] == 2:
                    for y in range(4):
                        for z in range(4):
                            at_row = c * 256 + z * 64 + y * 16
                            stacked[at_row:at_row + 16, first:first + width] = part[y, z]
                else:
                    stacked[c * 256:(c + 1) * 256, first:first + width] = dot(
                        swap(g), part.reshape(256, width)).astype(jnp.bfloat16)

        def tile(n, carry):
            cols = pl.ds(pl.multiple_of(n * 256, 256), 256)
            gate = dot(stacked[...], gate_v[:, cols])
            up = dot(stacked[...], up_v[:, cols])
            hidden[:, cols] = (gate / (1.0 + jnp.exp(-gate)) * up).astype(jnp.bfloat16)
            return carry

        lax.fori_loop(0, HIDDEN // 256, tile, 0)
        for g, (first, width, axes) in enumerate(GROUPS):
            result = dot(hidden[...], down_v[:, first:first + width]).astype(jnp.bfloat16)
            for i in (1, 2, 3):
                s2(g, q, i).wait_send()
            for c in (0, 1):
                half = result[c * 256:(c + 1) * 256]
                if axes[0] == 2:
                    half = half.reshape(4, 4, 16, width)
                    for y in range(4):
                        for z in range(4):
                            packed[g][q, c * 16 + y * 4 + z] = half[z, y]
                else:
                    packed[g][q, pl.ds(c * 16, 16)] = dot(swap(g), half).astype(jnp.bfloat16).reshape(16, 16, width)
            for i, d in PAIRS:
                r3(g, q, i, d).start()

    def back(q):
        for g, (first, width, axes) in enumerate(GROUPS):
            for i, d in PAIRS:
                copy = r3(g, q, i, d, near(axes[2], -i) * 2 + (core + d) % 2)
                if i == 0 and d == 0:
                    copy.wait()
                else:
                    copy.wait_recv()
            for i in (2, 1, 3, 0):
                r2(g, q, i).start()

    def combine(q):
        for g, (first, width, axes) in enumerate(GROUPS):
            for i in (1, 2, 3):
                r2(g, q, i, near(axes[1], -i)).wait_recv()
            r2(g, q, 0).wait()
            slot = slot_of[...] + (q * SLOTS).astype(jnp.float32)
            for v in range(SIDE):
                mix[v * TOK:(v + 1) * TOK, :] = jnp.where(
                    spread(v, ranks[g]) == slot, spread(v, weights[g]), 0.0).astype(jnp.bfloat16)
            total[g][...] += dot_tn(mix[...], back2[g][q].reshape(SIDE * TOK, width))

            @pl.when(q == ROUNDS - 1)
            def _():
                for i in (1, 2, 3):
                    s1(g, i).wait_send()
                blocks[g][...] = total[g][...].astype(jnp.bfloat16)
                for i in (2, 1, 3):
                    r1(g, i).start()

    def along_x():
        for i in range(1, 8):
            st(i, (rep + 8 - i) % 8).wait_recv()
        for i in (2, 1, 3):
            su(i).start()

    def across():
        for i in (1, 2, 3):
            su(i, near(2, -i)).wait_recv()
        sv().start()

    def shares():
        sv(1 - core).wait_recv()
        for r in range(8):
            for p in range(8):
                table[r * 256 + p * PIECE:r * 256 + (p + 1) * PIECE, :] = pieces[p, r]
        logits = dot(normed[...], table[...])
        eye = jnp.where(iota((TOK, TOK), 0) == iota((TOK, TOK), 1), 1.0, 0.0).astype(jnp.bfloat16)
        member = dot_nt(eye, members().astype(jnp.bfloat16))
        powers = jnp.where(member > 0.5, jnp.exp(logits), 0.0)
        share = (powers / jnp.sum(powers, axis=1, keepdims=True)).astype(jnp.bfloat16)
        for g, (first, width, axes) in enumerate(GROUPS):
            shares_out[g] = dot_nt(holder(g), share).astype(jnp.bfloat16)
            weights[g, :, lane(g)] = shares_out[g, pl.ds(pl.multiple_of(at[axes[0]] * 32, 32), 32), :]
        for g in range(3):
            for i in (2, 1, 3):
                sp(g, i).start()

    def prepare():
        for g, (first, width, axes) in enumerate(GROUPS):
            for i in (1, 2, 3):
                sp(g, i, near(axes[0], -i)).wait_recv()
            total[g][...] = jnp.zeros(total[g].shape, jnp.float32)

    for g, (first, width, axes) in enumerate(GROUPS):
        for i in (1, 2, 3):
            sq(g, i, near(axes[0], -i)).wait_recv()
            s1(g, i, near(axes[0], -i)).wait_recv()

    def step(k, carry):
        def stage(lag, run):
            @pl.when(jnp.logical_and(k >= lag, k < lag + ROUNDS))
            def _():
                run(k - lag)

        def once(when, run):
            @pl.when(k == when)
            def _():
                run()

        stage(0, gather)
        once(0, along_x)
        once(1, across)
        stage(1, forward)
        once(2, shares)

        @pl.when(k == 2)
        def _():
            for load in loads:
                load.wait()

        stage(2, expert)
        stage(3, back)
        once(3, prepare)
        stage(4, combine)
        return carry

    lax.fori_loop(0, ROUNDS + 4, step, 0)

    def leave(g):
        first, width, axes = GROUPS[g]
        return pltpu.make_async_copy(
            normed.at[:, first:first + width], out.at[:, first:first + width], out_sem.at[g])

    for g, (first, width, axes) in enumerate(GROUPS):
        result = total[g][own(g), :]
        for i in (1, 2, 3):
            r1(g, i).wait_recv()
            result = result + back1[g][i - 1].astype(jnp.float32)
        normed[:, first:first + width] = result.astype(jnp.bfloat16)
        leave(g).start()

    for i in (0, 1, 2, 3):
        (su(i) if i else sv()).wait_send()
    for i in range(1, 8):
        st(i).wait_send()
    for g in range(3):
        for i in (1, 2, 3):
            sq(g, i).wait_send()
            sp(g, i).wait_send()
            r1(g, i).wait_send()

    def drain(q, carry):
        for g in range(3):
            for i, d in PAIRS:
                if i or d:
                    s3(g, q, i, d).wait_send()
                    r3(g, q, i, d).wait_send()
            for i in (1, 2, 3):
                r2(g, q, i).wait_send()
        return carry

    lax.fori_loop(0, ROUNDS, drain, 0)
    for g in range(3):
        leave(g).wait()


def per_group(shape):
    return [pltpu.VMEM(shape(width), jnp.bfloat16) for _, width, _ in GROUPS]


def flat_kernel(*refs):
    args, rest = refs[:9], list(refs[9:])

    def take(n):
        head = rest[:n]
        del rest[:n]
        return head

    blocks = take(3)
    ranks, weights = take(2)
    packed, hop2, arrived, back3, back2, back1, total = (take(3) for _ in range(7))
    kernel(*args, blocks, ranks, weights, packed, hop2, arrived, back3, back2, back1, total, *rest)


def per_device(tokens, norm_gain, router, routes, placement, w_gate, w_up, w_down):
    dma = pltpu.SemaphoreType.DMA
    bf = jnp.bfloat16
    scratch = (
        per_group(lambda w: (SIDE * TOK, w))
        + [pltpu.VMEM((3, 32, SIDE * TOK), bf), pltpu.VMEM((3, 32, SIDE * TOK), bf)]
        + per_group(lambda w: (ROUNDS, 32, 16, w))
        + per_group(lambda w: (ROUNDS, 4, 8, 16, w))
        + per_group(lambda w: (ROUNDS, 8, 4, 16, w))
        + per_group(lambda w: (ROUNDS, 4, 8, 16, w))
        + per_group(lambda w: (ROUNDS, 4, 8, 16, w))
        + per_group(lambda w: (3, TOK, w))
        + [pltpu.VMEM((SIDE * TOK, w), jnp.float32) for _, w, _ in GROUPS]
        + [
            pltpu.VMEM((WIDTH, HIDDEN), bf),
            pltpu.VMEM((WIDTH, HIDDEN), bf),
            pltpu.VMEM((HIDDEN, WIDTH), bf),
            pltpu.VMEM((TOK, WIDTH), bf),
            pltpu.VMEM((WIDTH, DEVICES), bf),
            pltpu.VMEM((8, 8, PIECE, DEVICES), bf),
            pltpu.VMEM((SIDE * TOK, WIDTH), bf),
            pltpu.VMEM((SIDE * TOK, HIDDEN), bf),
            pltpu.VMEM((TOK, SIDE * TOK), jnp.float32),
            pltpu.VMEM((SIDE * TOK, SIDE * TOK), bf),
            pltpu.VMEM((TOK, WIDTH), bf),
            pltpu.VMEM((1, WIDTH), jnp.float32),
            pltpu.VMEM((8, TOK), jnp.int32),
            pltpu.VMEM((1, DEVICES), jnp.int32),
            pltpu.VMEM((3, DEVICES, TOK), bf),
            pltpu.VMEM((3, DEVICES, TOK), bf),
            dma((3,)), dma((5,)), dma((3,)),
            dma((8,)), dma((8,)),
            dma((4,)), dma((4,)),
            dma((3, 4)), dma((3, 4)),
            dma((3, 4)), dma((3, 4)),
            dma((3, 4)), dma((3, 4)),
            dma((3, ROUNDS, 4)), dma((3, ROUNDS, 4)),
            dma((3, ROUNDS, 8)), dma((3, ROUNDS, 8)),
            dma((3, ROUNDS, 8)), dma((3, ROUNDS, 8)),
            dma((3, ROUNDS, 4)), dma((3, ROUNDS, 4)),
            dma((3, 4)), dma((3, 4)),
        ]
    )
    whole = pl.BlockSpec(memory_space=pl.ANY)
    return pl.pallas_call(
        flat_kernel,
        name="moe",
        out_shape=jax.ShapeDtypeStruct((TOK, WIDTH), bf),
        in_specs=[whole] * 8,
        out_specs=whole,
        scratch_shapes=scratch,
        compiler_params=pltpu.CompilerParams(
            collective_id=0, has_side_effects=True, vmem_limit_bytes=63 * 2**20
        ),
        cost_estimate=pl.CostEstimate(flops=15 * 10**9, bytes_accessed=11 * 10**6, transcendentals=10**6),
    )(tokens, norm_gain.reshape(1, WIDTH), router, routes.T, placement.reshape(1, DEVICES), w_gate, w_up, w_down)


def solution(mesh):
    placed = (
        P(("rep", "expert"), None),
        P(),
        P("rep", None),
        P(("rep", "expert"), None),
        P(),
        P(("rep", "expert"), None, None),
        P(("rep", "expert"), None, None),
        P(("rep", "expert"), None, None),
    )
    return jax.shard_map(
        per_device,
        mesh=mesh,
        in_specs=placed,
        out_specs=P(("rep", "expert"), None),
        check_vma=False,
    )
```

```python
import jax
import jax.numpy as jnp
from jax import lax
from jax.experimental import pallas as pl
from jax.experimental.pallas import tpu as pltpu
from jax.sharding import PartitionSpec as P

MESH = pl.DeviceIdType.MESH
TOK = 128
WIDTH = 2048
HIDDEN = 768
SIDE = 4
ROUNDS = 3
SLOTS = 4
DEVICES = 128
GROUPS = (
    (0, 768, (2, 0, 1)),
    (768, 640, (0, 1, 2)),
    (1408, 640, (1, 2, 0)),
)
NT = (((1,), (1,)), ((), ()))
TN = (((0,), (0,)), ((), ()))
PIECE = 32


def iota(shape, dim):
    return lax.broadcasted_iota(jnp.int32, shape, dim)


def dot(a, b):
    return jnp.dot(a, b, preferred_element_type=jnp.float32)


def dot_nt(a, b):
    return lax.dot_general(a, b, NT, preferred_element_type=jnp.float32)


def dot_tn(a, b):
    return lax.dot_general(a, b, TN, preferred_element_type=jnp.float32)


def kernel(
    tokens, gain, router, routes, placement, w_gate, w_up, w_down, own_out, parts,
    blocks, ranks, weights, packed, hop2, arrived, back3, back2, total,
    gate_v, up_v, down_v, normed, table, pieces, stacked, hidden, slot_of, mix,
    tokens_v, gain_v, routes_v, placement_v, ranks_out, shares_out,
    w_sem, in_sem, out_sem, t_send, t_recv, u_send, u_recv,
    s1_send, s1_recv, q_send, q_recv, p_send, p_recv, s2_send, s2_recv, s3_send, s3_recv, r3_send, r3_recv, r2_send, r2_recv, r1_send, r1_recv,
):
    rep = lax.axis_index("rep")
    exp = lax.axis_index("expert")
    core = exp % 2
    at = (rep // 2, (rep % 2) * 2 + exp // 8, (exp // 2) % 4)

    def device(pos, c):
        z, y, x = pos
        return (z * 2 + y // 2, (y % 2) * 8 + x * 2 + c)

    def along(axis, value, c):
        pos = list(at)
        pos[axis] = value
        return device(pos, c)

    def near(axis, step):
        return (at[axis] + step) % SIDE

    def remote(src, dst, send, recv, dev):
        return pltpu.make_async_remote_copy(
            src_ref=src, dst_ref=dst, send_sem=send, recv_sem=recv,
            device_id=dev, device_id_type=MESH,
        )

    def came(ref, sem):
        remote(ref, ref, sem, sem, device(at, 1 - core)).wait_recv()

    def went(ref, sem):
        remote(ref, ref, sem, sem, device(at, 1 - core)).wait_send()

    barrier = pltpu.get_barrier_semaphore()
    greeted = [along(a, near(a, i), (core + d) % 2) for a in range(3) for i in (1, 2, 3) for d in (0, 1)]
    greeted.append(device(at, 1 - core))
    greeted += [device((near(0, i), near(1, 2), at[2]), core) for i in (1, 2, 3)]
    for dev in greeted:
        pl.semaphore_signal(barrier, inc=1, device_id=dev, device_id_type=MESH)

    mine = core * 4 + at[2]
    operands = [
        pltpu.make_async_copy(tokens, tokens_v, in_sem.at[0]),
        pltpu.make_async_copy(gain, gain_v, in_sem.at[1]),
        pltpu.make_async_copy(routes, routes_v, in_sem.at[2]),
        pltpu.make_async_copy(placement, placement_v, in_sem.at[3]),
        pltpu.make_async_copy(
            router.at[pl.ds(pl.multiple_of(mine * PIECE, PIECE), PIECE)], pieces.at[mine, rep], in_sem.at[4]),
    ]
    for load in operands:
        load.start()
    loads = [
        pltpu.make_async_copy(w_gate.at[0], gate_v, w_sem.at[0]),
        pltpu.make_async_copy(w_up.at[0], up_v, w_sem.at[1]),
        pltpu.make_async_copy(w_down.at[0], down_v, w_sem.at[2]),
    ]
    for load in loads:
        load.start()

    operands[0].wait()
    operands[1].wait()
    values = tokens_v[...].astype(jnp.float32)
    scale = lax.rsqrt(jnp.mean(values * values, axis=-1, keepdims=True) + 1e-06)
    normed[...] = (values * scale * gain_v[...]).astype(jnp.bfloat16)
    for g, (first, width, axes) in enumerate(GROUPS):
        blocks[g][pl.ds(pl.multiple_of(at[axes[0]] * TOK, TOK), TOK), :] = normed[:, first:first + width]

    def holder(g):
        a1, a2, a3 = GROUPS[g][2]
        r = iota((DEVICES, DEVICES), 0)
        pos = [None, None, None]
        pos[a1] = r // 32
        pos[a2] = (r // 8) % 4
        pos[a3] = (r // 2) % 4
        wanted = pos[0] * 32 + pos[1] * 8 + pos[2] * 2 + r % 2
        return jnp.where(placement_v[...] == wanted, 1.0, 0.0).astype(jnp.bfloat16)

    def members():
        found = jnp.zeros((DEVICES, TOK), jnp.float32)
        rows = iota((DEVICES, TOK), 0)
        for k in range(8):
            found = found + jnp.where(routes_v[k:k + 1, :] == rows, 1.0, 0.0)
        return found

    operands[2].wait()
    operands[3].wait()
    member = members()
    before = jnp.where(iota((TOK, TOK), 0) < iota((TOK, TOK), 1), 1.0, 0.0).astype(jnp.bfloat16)
    rank = jnp.where(member > 0.5, dot(member.astype(jnp.bfloat16), before), -1.0).astype(jnp.bfloat16)
    for g, (first, width, axes) in enumerate(GROUPS):
        ranks_out[g] = dot(holder(g), rank).astype(jnp.bfloat16)
        ranks[g, :, pl.ds(pl.multiple_of(at[axes[0]] * TOK, TOK), TOK)] = ranks_out[
            g, pl.ds(pl.multiple_of(at[axes[0]] * 32, 32), 32), :]
    operands[4].wait()

    pl.semaphore_wait(barrier, len(greeted))

    def block(g, position):
        return pl.ds(pl.multiple_of(position * TOK, TOK), TOK)

    def own(g):
        return block(g, at[GROUPS[g][2][0]])

    def s1(g, i):
        a = GROUPS[g][2][0]
        return remote(blocks[g].at[own(g)], blocks[g].at[own(g)], s1_send.at[g], s1_recv.at[g],
                      along(a, near(a, i), core))

    def sq(g, i):
        a = GROUPS[g][2][0]
        v = near(a, i)
        return remote(ranks_out.at[g, pl.ds(pl.multiple_of(v * 32, 32), 32)], ranks.at[g, :, own(g)],
                      q_send.at[0], q_recv.at[0], along(a, v, core))

    def sp(g, i):
        a = GROUPS[g][2][0]
        v = near(a, i)
        return remote(shares_out.at[g, pl.ds(pl.multiple_of(v * 32, 32), 32)], weights.at[g, :, own(g)],
                      p_send.at[0], p_recv.at[0], along(a, v, core))

    def st(i):
        return remote(pieces.at[mine, rep], pieces.at[mine, rep],
                      t_send.at[0], t_recv.at[0], ((rep + i) % 8, exp))

    def su(i):
        return remote(pieces.at[mine], pieces.at[mine],
                      u_send.at[1], u_recv.at[1], along(2, near(2, i), core))

    def sv():
        return remote(pieces.at[pl.ds(core * 4, 4)], pieces.at[pl.ds(core * 4, 4)],
                      u_send.at[0], u_recv.at[0], device(at, 1 - core))

    for i in (2, 1, 3):
        for g in range(3):
            s1(g, i).start()
    for g in range(3):
        for i in (2, 1, 3):
            sq(g, i).start()
    for i in range(1, 8):
        st(i).start()

    row = iota((TOK, SIDE * TOK), 0)
    col = iota((TOK, SIDE * TOK), 1)
    slot_of[...] = jnp.where((row // 4) % 4 == col // TOK, row % 4, 1000).astype(jnp.float32)

    def spread(v, plane):
        r = iota((TOK, 32), 0)
        pick = jnp.where(iota((TOK, 32), 1) == v * 8 + r // 16, 1.0, 0.0).astype(jnp.bfloat16)
        return dot(pick, plane)

    def swap(g):
        r = iota((256, 256), 0)
        c = iota((256, 256), 1)
        a, b, d, s = r // 64, (r // 16) % 4, (r // 4) % 4, r % 4
        if GROUPS[g][2][0] == 0:
            wanted = d * 64 + b * 16 + a * 4 + s
        else:
            wanted = a * 64 + d * 16 + b * 4 + s
        return jnp.where(c == wanted, 1.0, 0.0).astype(jnp.bfloat16)

    def s2(g, q, i):
        a = GROUPS[g][2][1]
        v = near(a, i)
        return remote(packed[g].at[q, pl.ds(v * 8, 8)], hop2[g].at[q, at[a]],
                      s2_send.at[g, q], s2_recv.at[g, q], along(a, v, core))

    def s3(g, q, i, d):
        a = GROUPS[g][2][2]
        u, c = near(a, i), (core + d) % 2
        src = hop2[g].at[q, :, u * 2 + c]
        dst = arrived[g].at[q, core * 4 + at[a]]
        if i == 0 and d == 0:
            return pltpu.make_async_copy(src, dst, s3_recv.at[g, q])
        return remote(src, dst, s3_send.at[g], s3_recv.at[g, q], along(a, u, c))

    def r3(g, q, i, d):
        a = GROUPS[g][2][2]
        u, c = near(a, i), (core + d) % 2
        src = packed[g].at[q, pl.ds((c * 4 + u) * 4, 4)]
        dst = back3[g].at[q, :, at[a] * 2 + core]
        if i == 0 and d == 0:
            return pltpu.make_async_copy(src, dst, r3_recv.at[g, q])
        return remote(src, dst, r3_send.at[g], r3_recv.at[g, q], along(a, u, c))

    def r2(g, q, i):
        a = GROUPS[g][2][1]
        v = near(a, i)
        src, dst = back3[g].at[q, v], back2[g].at[q, at[a]]
        if i == 0:
            return pltpu.make_async_copy(src, dst, r2_recv.at[g, q])
        return remote(src, dst, r2_send.at[g], r2_recv.at[g, q], along(a, v, core))

    def r1(g, i):
        first, width, axes = GROUPS[g]
        a = axes[0]
        return remote(blocks[g].at[block(g, near(a, i))], parts.at[i - 1, :, first:first + width], r1_send.at[g], r1_recv.at[g],
                      along(a, near(a, i), core))

    PAIRS = [(i, d) for i in (2, 1, 3, 0) for d in (0, 1)]

    def gather(q):
        slot = slot_of[...] + (q * SLOTS).astype(jnp.float32)
        for i in (2, 1, 3, 0):
            for g, (first, width, axes) in enumerate(GROUPS):
                v = near(axes[1], i)
                found = spread(v, ranks[g])
                pick = jnp.where(found == slot, 1.0, 0.0).astype(jnp.bfloat16)
                rows = dot(pick, blocks[g][...]).astype(jnp.bfloat16).reshape(8, 16, width)
                if i == 0:
                    hop2[g][q, v] = rows
                else:
                    packed[g][q, pl.ds(v * 8, 8)] = rows
                    s2(g, q, i).start()

    def forward(q):
        for g in range(3):
            came(hop2[g].at[q, pl.ds(0, 3)], s2_recv.at[g, q])
            for i, d in PAIRS:
                s3(g, q, i, d).start()

    def expert(q):
        for g, (first, width, axes) in enumerate(GROUPS):
            came(arrived[g].at[q], s3_recv.at[g, q])
            for c in (0, 1):
                part = arrived[g][q, pl.ds(c * 4, 4)]
                if axes[0] == 2:
                    for y in range(4):
                        for z in range(4):
                            at_row = c * 256 + z * 64 + y * 16
                            stacked[at_row:at_row + 16, first:first + width] = part[y, z]
                else:
                    stacked[c * 256:(c + 1) * 256, first:first + width] = dot(
                        swap(g), part.reshape(256, width)).astype(jnp.bfloat16)

        def tile(n, carry):
            cols = pl.ds(pl.multiple_of(n * 256, 256), 256)
            gate = dot(stacked[...], gate_v[:, cols])
            up = dot(stacked[...], up_v[:, cols])
            hidden[:, cols] = (gate / (1.0 + jnp.exp(-gate)) * up).astype(jnp.bfloat16)
            return carry

        lax.fori_loop(0, HIDDEN // 256, tile, 0)
        for g, (first, width, axes) in enumerate(GROUPS):
            result = dot(hidden[...], down_v[:, first:first + width]).astype(jnp.bfloat16)
            went(packed[g].at[q, pl.ds(0, 24)], s2_send.at[g, q])
            for c in (0, 1):
                half = result[c * 256:(c + 1) * 256]
                if axes[0] == 2:
                    half = half.reshape(4, 4, 16, width)
                    for y in range(4):
                        for z in range(4):
                            packed[g][q, c * 16 + y * 4 + z] = half[z, y]
                else:
                    packed[g][q, pl.ds(c * 16, 16)] = dot(swap(g), half).astype(jnp.bfloat16).reshape(16, 16, width)
            for i, d in PAIRS:
                r3(g, q, i, d).start()

    def back(q):
        for g, (first, width, axes) in enumerate(GROUPS):
            came(back3[g].at[q], r3_recv.at[g, q])
            for i in (2, 1, 3, 0):
                r2(g, q, i).start()

    def leave(g):
        first, width, axes = GROUPS[g]
        return pltpu.make_async_copy(
            total[g].at[own(g)], own_out.at[:, first:first + width], out_sem.at[g])

    def combine(q):
        slot = slot_of[...] + (q * SLOTS).astype(jnp.float32)
        for g in range(3):
            for v in range(SIDE):
                mix[g, v * TOK:(v + 1) * TOK, :] = jnp.where(
                    spread(v, ranks[g]) == slot, spread(v, weights[g]), 0.0).astype(jnp.bfloat16)
        for g, (first, width, axes) in enumerate(GROUPS):
            came(back2[g].at[q], r2_recv.at[g, q])
            total[g][...] += dot_tn(mix[g], back2[g][q].reshape(SIDE * TOK, width))

            @pl.when(q == ROUNDS - 1)
            def _():
                went(blocks[g].at[pl.ds(0, 3 * TOK)], s1_send.at[g])
                blocks[g][...] = total[g][...].astype(jnp.bfloat16)
                for i in (2, 1, 3):
                    r1(g, i).start()
                leave(g).start()

    def along_x():
        came(pieces.at[mine, pl.ds(0, 7)], t_recv.at[0])
        for i in (2, 1, 3):
            su(i).start()

    def across():
        came(pieces.at[pl.ds(0, 3)], u_recv.at[1])
        sv().start()

    def shares():
        came(pieces.at[pl.ds(0, 4)], u_recv.at[0])
        for r in range(8):
            for p in range(8):
                table[r * 256 + p * PIECE:r * 256 + (p + 1) * PIECE, :] = pieces[p, r]
        logits = dot(normed[...], table[...])
        eye = jnp.where(iota((TOK, TOK), 0) == iota((TOK, TOK), 1), 1.0, 0.0).astype(jnp.bfloat16)
        member = dot_nt(eye, members().astype(jnp.bfloat16))
        powers = jnp.where(member > 0.5, jnp.exp(logits), 0.0)
        share = (powers / jnp.sum(powers, axis=1, keepdims=True)).astype(jnp.bfloat16)
        for g, (first, width, axes) in enumerate(GROUPS):
            shares_out[g] = dot_nt(holder(g), share).astype(jnp.bfloat16)
            weights[g, :, own(g)] = shares_out[g, pl.ds(pl.multiple_of(at[axes[0]] * 32, 32), 32), :]
        for g in range(3):
            for i in (2, 1, 3):
                sp(g, i).start()

    def prepare():
        came(weights.at[:, :, pl.ds(0, 3 * TOK)], p_recv.at[0])
        for g in range(3):
            total[g][...] = jnp.zeros(total[g].shape, jnp.float32)

    came(ranks.at[:, :, pl.ds(0, 3 * TOK)], q_recv.at[0])
    for g in range(3):
        came(blocks[g].at[pl.ds(0, 3 * TOK)], s1_recv.at[g])

    def step(k, carry):
        def stage(lag, run):
            @pl.when(jnp.logical_and(k >= lag, k < lag + ROUNDS))
            def _():
                run(k - lag)

        def once(when, run):
            @pl.when(k == when)
            def _():
                run()

        stage(0, gather)
        once(0, along_x)
        once(1, across)
        stage(1, forward)
        once(2, shares)

        @pl.when(k == 2)
        def _():
            for load in loads:
                load.wait()

        stage(2, expert)
        stage(3, back)
        once(3, prepare)
        stage(4, combine)
        return carry

    lax.fori_loop(0, ROUNDS + 4, step, 0)

    for g, (first, width, axes) in enumerate(GROUPS):
        came(parts.at[:, :, first:first + width], r1_recv.at[g])
    went(pieces.at[pl.ds(0, 4)], u_send.at[0])
    went(pieces.at[pl.ds(0, 3)], u_send.at[1])
    went(pieces.at[0, pl.ds(0, 7)], t_send.at[0])
    went(ranks.at[:, :, pl.ds(0, 3 * TOK)], q_send.at[0])
    went(weights.at[:, :, pl.ds(0, 3 * TOK)], p_send.at[0])
    for g in range(3):
        went(hop2[g].at[:, :, pl.ds(0, 7)], s3_send.at[g])
        went(hop2[g].at[:, :, pl.ds(0, 7)], r3_send.at[g])
        went(back3[g].at[:, pl.ds(0, 3)], r2_send.at[g])
        went(blocks[g].at[pl.ds(0, 3 * TOK)], r1_send.at[g])
        leave(g).wait()


def per_group(shape):
    return [pltpu.VMEM(shape(width), jnp.bfloat16) for _, width, _ in GROUPS]


def flat_kernel(*refs):
    args, rest = refs[:10], list(refs[10:])

    def take(n):
        head = rest[:n]
        del rest[:n]
        return head

    blocks = take(3)
    ranks, weights = take(2)
    packed, hop2, arrived, back3, back2, total = (take(3) for _ in range(6))
    kernel(*args, blocks, ranks, weights, packed, hop2, arrived, back3, back2, total, *rest)


def per_device(tokens, norm_gain, router, routes, placement, w_gate, w_up, w_down):
    dma = pltpu.SemaphoreType.DMA
    bf = jnp.bfloat16
    scratch = (
        per_group(lambda w: (SIDE * TOK, w))
        + [pltpu.VMEM((3, 32, SIDE * TOK), bf), pltpu.VMEM((3, 32, SIDE * TOK), bf)]
        + per_group(lambda w: (ROUNDS, 32, 16, w))
        + per_group(lambda w: (ROUNDS, 4, 8, 16, w))
        + per_group(lambda w: (ROUNDS, 8, 4, 16, w))
        + per_group(lambda w: (ROUNDS, 4, 8, 16, w))
        + per_group(lambda w: (ROUNDS, 4, 8, 16, w))
        + [pltpu.VMEM((SIDE * TOK, w), jnp.float32) for _, w, _ in GROUPS]
        + [
            pltpu.VMEM((WIDTH, HIDDEN), bf),
            pltpu.VMEM((WIDTH, HIDDEN), bf),
            pltpu.VMEM((HIDDEN, WIDTH), bf),
            pltpu.VMEM((TOK, WIDTH), bf),
            pltpu.VMEM((WIDTH, DEVICES), bf),
            pltpu.VMEM((8, 8, PIECE, DEVICES), bf),
            pltpu.VMEM((SIDE * TOK, WIDTH), bf),
            pltpu.VMEM((SIDE * TOK, HIDDEN), bf),
            pltpu.VMEM((TOK, SIDE * TOK), jnp.float32),
            pltpu.VMEM((3, SIDE * TOK, SIDE * TOK), bf),
            pltpu.VMEM((TOK, WIDTH), bf),
            pltpu.VMEM((1, WIDTH), jnp.float32),
            pltpu.VMEM((8, TOK), jnp.int32),
            pltpu.VMEM((1, DEVICES), jnp.int32),
            pltpu.VMEM((3, DEVICES, TOK), bf),
            pltpu.VMEM((3, DEVICES, TOK), bf),
            dma((3,)), dma((5,)), dma((3,)),
            dma((1,)), dma((1,)),
            dma((2,)), dma((2,)),
            dma((3,)), dma((3,)),
            dma((1,)), dma((1,)),
            dma((1,)), dma((1,)),
            dma((3, ROUNDS)), dma((3, ROUNDS)),
            dma((3,)), dma((3, ROUNDS)),
            dma((3,)), dma((3, ROUNDS)),
            dma((3,)), dma((3, ROUNDS)),
            dma((3,)), dma((3,)),
        ]
    )
    whole = pl.BlockSpec(memory_space=pl.ANY)
    own_part, parts = pl.pallas_call(
        flat_kernel,
        name="moe",
        out_shape=(
            jax.ShapeDtypeStruct((TOK, WIDTH), jnp.float32),
            jax.ShapeDtypeStruct((3, TOK, WIDTH), bf),
        ),
        in_specs=[whole] * 8,
        out_specs=(whole, whole),
        scratch_shapes=scratch,
        compiler_params=pltpu.CompilerParams(
            collective_id=0, has_side_effects=True, vmem_limit_bytes=63 * 2**20
        ),
        cost_estimate=pl.CostEstimate(flops=15 * 10**9, bytes_accessed=11 * 10**6, transcendentals=10**6),
    )(tokens, norm_gain.reshape(1, WIDTH), router, routes.T, placement.reshape(1, DEVICES), w_gate, w_up, w_down)
    one, two, three = (parts[i].astype(jnp.float32) for i in range(3))
    return (own_part + one + two + three).astype(bf)


def solution(mesh):
    placed = (
        P(("rep", "expert"), None),
        P(),
        P("rep", None),
        P(("rep", "expert"), None),
        P(),
        P(("rep", "expert"), None, None),
        P(("rep", "expert"), None, None),
        P(("rep", "expert"), None, None),
    )
    return jax.shard_map(
        per_device,
        mesh=mesh,
        in_specs=placed,
        out_specs=P(("rep", "expert"), None),
        check_vma=False,
    )
```

```python
import jax
import jax.numpy as jnp
from jax import lax
from jax.experimental import pallas as pl
from jax.experimental.pallas import tpu as pltpu
from jax.sharding import PartitionSpec as P

MESH = pl.DeviceIdType.MESH
TOK = 128
WIDTH = 2048
HIDDEN = 768
SIDE = 4
ROUNDS = 3
SLOTS = 4
DEVICES = 128
GROUPS = (
    (0, 768, (2, 0, 1)),
    (768, 640, (0, 1, 2)),
    (1408, 640, (1, 2, 0)),
)
NT = (((1,), (1,)), ((), ()))
TN = (((0,), (0,)), ((), ()))
PIECE = 32
HALF = 384


def iota(shape, dim):
    return lax.broadcasted_iota(jnp.int32, shape, dim)


def dot(a, b):
    return jnp.dot(a, b, preferred_element_type=jnp.float32)


def dot_nt(a, b):
    return lax.dot_general(a, b, NT, preferred_element_type=jnp.float32)


def dot_tn(a, b):
    return lax.dot_general(a, b, TN, preferred_element_type=jnp.float32)


def kernel(
    tokens, gain, router, routes, placement, w_gate, w_up, w_down, parts,
    blocks, ranks, weights, packed, hop2, arrived, back3, back2, total,
    gate_v, up_v, down_v, normed, table, pieces, stacked, hidden, slot_of, mix,
    tokens_v, gain_v, routes_v, placement_v, ranks_out, shares_out,
    w_sem, in_sem, out_sem, t_send, t_recv, u_send, u_recv,
    s1_send, s1_recv, q_send, q_recv, p_send, p_recv, s2_send, s2_recv, s3_send, s3_recv, r3_send, r3_recv, r2_send, r2_recv, r1_send, r1_recv,
):
    rep = lax.axis_index("rep")
    exp = lax.axis_index("expert")
    core = exp % 2
    at = (rep // 2, (rep % 2) * 2 + exp // 8, (exp // 2) % 4)

    def device(pos, c):
        z, y, x = pos
        return (z * 2 + y // 2, (y % 2) * 8 + x * 2 + c)

    def along(axis, value, c):
        pos = list(at)
        pos[axis] = value
        return device(pos, c)

    def near(axis, step):
        return (at[axis] + step) % SIDE

    def remote(src, dst, send, recv, dev):
        return pltpu.make_async_remote_copy(
            src_ref=src, dst_ref=dst, send_sem=send, recv_sem=recv,
            device_id=dev, device_id_type=MESH,
        )

    def came(ref, sem):
        remote(ref, ref, sem, sem, device(at, 1 - core)).wait_recv()

    def went(ref, sem):
        remote(ref, ref, sem, sem, device(at, 1 - core)).wait_send()

    barrier = pltpu.get_barrier_semaphore()
    greeted = [along(a, near(a, i), (core + d) % 2) for a in range(3) for i in (1, 2, 3) for d in (0, 1)]
    greeted.append(device(at, 1 - core))
    greeted += [device((near(0, i), near(1, 2), at[2]), core) for i in (1, 2, 3)]
    for dev in greeted:
        pl.semaphore_signal(barrier, inc=1, device_id=dev, device_id_type=MESH)

    mine = core * 4 + at[2]
    operands = [
        pltpu.make_async_copy(tokens, tokens_v, in_sem.at[0]),
        pltpu.make_async_copy(gain, gain_v, in_sem.at[1]),
        pltpu.make_async_copy(routes, routes_v, in_sem.at[2]),
        pltpu.make_async_copy(placement, placement_v, in_sem.at[3]),
        pltpu.make_async_copy(
            router.at[pl.ds(pl.multiple_of(mine * PIECE, PIECE), PIECE)], pieces.at[mine, rep], in_sem.at[4]),
    ]
    for load in operands:
        load.start()
    loads = [
        pltpu.make_async_copy(w_gate.at[0], gate_v, w_sem.at[0]),
        pltpu.make_async_copy(w_up.at[0], up_v, w_sem.at[1]),
        pltpu.make_async_copy(w_down.at[0], down_v, w_sem.at[2]),
    ]
    for load in loads:
        load.start()

    operands[0].wait()
    operands[1].wait()
    values = tokens_v[...].astype(jnp.float32)
    scale = lax.rsqrt(jnp.mean(values * values, axis=-1, keepdims=True) + 1e-06)
    normed[...] = (values * scale * gain_v[...]).astype(jnp.bfloat16)
    for g, (first, width, axes) in enumerate(GROUPS):
        blocks[g][pl.ds(pl.multiple_of(at[axes[0]] * TOK, TOK), TOK), :] = normed[:, first:first + width]

    def holder(g):
        a1, a2, a3 = GROUPS[g][2]
        r = iota((DEVICES, DEVICES), 0)
        pos = [None, None, None]
        pos[a1] = r // 32
        pos[a2] = (r // 8) % 4
        pos[a3] = (r // 2) % 4
        wanted = pos[0] * 32 + pos[1] * 8 + pos[2] * 2 + r % 2
        return jnp.where(placement_v[...] == wanted, 1.0, 0.0).astype(jnp.bfloat16)

    def members():
        found = jnp.zeros((DEVICES, TOK), jnp.float32)
        rows = iota((DEVICES, TOK), 0)
        for k in range(8):
            found = found + jnp.where(routes_v[k:k + 1, :] == rows, 1.0, 0.0)
        return found

    operands[2].wait()
    operands[3].wait()
    member = members()
    before = jnp.where(iota((TOK, TOK), 0) < iota((TOK, TOK), 1), 1.0, 0.0).astype(jnp.bfloat16)
    rank = jnp.where(member > 0.5, dot(member.astype(jnp.bfloat16), before), -1.0).astype(jnp.bfloat16)
    for g, (first, width, axes) in enumerate(GROUPS):
        ranks_out[g] = dot(holder(g), rank).astype(jnp.bfloat16)
        ranks[g, :, pl.ds(pl.multiple_of(at[axes[0]] * TOK, TOK), TOK)] = ranks_out[
            g, pl.ds(pl.multiple_of(at[axes[0]] * 32, 32), 32), :]
    operands[4].wait()

    pl.semaphore_wait(barrier, len(greeted))

    def block(g, position):
        return pl.ds(pl.multiple_of(position * TOK, TOK), TOK)

    def own(g):
        return block(g, at[GROUPS[g][2][0]])

    def half(g, h):
        return slice(0, HALF) if h == 0 else slice(HALF, GROUPS[g][1])

    def s1(g, i, h):
        a = GROUPS[g][2][0]
        mine = blocks[g].at[own(g), half(g, h)]
        return remote(mine, mine, s1_send.at[g], s1_recv.at[g, h],
                      along(a, near(a, i), core))

    def sq(g, i):
        a = GROUPS[g][2][0]
        v = near(a, i)
        return remote(ranks_out.at[g, pl.ds(pl.multiple_of(v * 32, 32), 32)], ranks.at[g, :, own(g)],
                      q_send.at[0], q_recv.at[0], along(a, v, core))

    def sp(g, i):
        a = GROUPS[g][2][0]
        v = near(a, i)
        return remote(shares_out.at[g, pl.ds(pl.multiple_of(v * 32, 32), 32)], weights.at[g, :, own(g)],
                      p_send.at[0], p_recv.at[0], along(a, v, core))

    def st(i):
        return remote(pieces.at[mine, rep], pieces.at[mine, rep],
                      t_send.at[0], t_recv.at[0], ((rep + i) % 8, exp))

    def su(i):
        return remote(pieces.at[mine], pieces.at[mine],
                      u_send.at[1], u_recv.at[1], along(2, near(2, i), core))

    def sv():
        return remote(pieces.at[pl.ds(core * 4, 4)], pieces.at[pl.ds(core * 4, 4)],
                      u_send.at[0], u_recv.at[0], device(at, 1 - core))

    for i in (2, 1, 3):
        for g in range(3):
            s1(g, i, 0).start()
    for g in range(3):
        for i in (2, 1, 3):
            sq(g, i).start()
    for i in (2, 1, 3):
        for g in range(3):
            s1(g, i, 1).start()
    for i in range(1, 8):
        st(i).start()

    row = iota((TOK, SIDE * TOK), 0)
    col = iota((TOK, SIDE * TOK), 1)
    slot_of[...] = jnp.where((row // 4) % 4 == col // TOK, row % 4, 1000).astype(jnp.float32)

    def spread(v, plane):
        r = iota((TOK, 32), 0)
        pick = jnp.where(iota((TOK, 32), 1) == v * 8 + r // 16, 1.0, 0.0).astype(jnp.bfloat16)
        return dot(pick, plane)

    def swap(g):
        r = iota((256, 256), 0)
        c = iota((256, 256), 1)
        a, b, d, s = r // 64, (r // 16) % 4, (r // 4) % 4, r % 4
        if GROUPS[g][2][0] == 0:
            wanted = d * 64 + b * 16 + a * 4 + s
        else:
            wanted = a * 64 + d * 16 + b * 4 + s
        return jnp.where(c == wanted, 1.0, 0.0).astype(jnp.bfloat16)

    def s2(g, q, i, cols):
        a = GROUPS[g][2][1]
        v = near(a, i)
        return remote(packed[g].at[q, pl.ds(v * 8, 8), :, cols], hop2[g].at[q, at[a], :, :, cols],
                      s2_send.at[g, q], s2_recv.at[g, q], along(a, v, core))

    def s3(g, q, i, d):
        a = GROUPS[g][2][2]
        u, c = near(a, i), (core + d) % 2
        src = hop2[g].at[q, :, u * 2 + c]
        dst = arrived[g].at[q, core * 4 + at[a]]
        if i == 0 and d == 0:
            return pltpu.make_async_copy(src, dst, s3_recv.at[g, q])
        return remote(src, dst, s3_send.at[g], s3_recv.at[g, q], along(a, u, c))

    def r3(g, q, i, d):
        a = GROUPS[g][2][2]
        u, c = near(a, i), (core + d) % 2
        src = packed[g].at[q, pl.ds((c * 4 + u) * 4, 4)]
        dst = back3[g].at[q, :, at[a] * 2 + core]
        if i == 0 and d == 0:
            return pltpu.make_async_copy(src, dst, r3_recv.at[g, q])
        return remote(src, dst, r3_send.at[g], r3_recv.at[g, q], along(a, u, c))

    def r2(g, q, i, h):
        a = GROUPS[g][2][1]
        v = near(a, i)
        cols = half(g, h)
        src, dst = back3[g].at[q, v, :, :, cols], back2[g].at[q, at[a], :, :, cols]
        if i == 0:
            return pltpu.make_async_copy(src, dst, r2_recv.at[g, q, h])
        return remote(src, dst, r2_send.at[g], r2_recv.at[g, q, h], along(a, v, core))

    def r1(g, i, h):
        first, width, axes = GROUPS[g]
        a = axes[0]
        cols = half(g, h)
        return remote(blocks[g].at[block(g, near(a, i)), cols],
                      parts.at[i - 1, :, first + cols.start:first + cols.stop], r1_send.at[g], r1_recv.at[g],
                      along(a, near(a, i), core))

    PAIRS = [(i, d) for i in (2, 1, 3, 0) for d in (0, 1)]

    def choose(q):
        slot = slot_of[...] + jnp.asarray(q * SLOTS, jnp.float32)
        for i in range(SIDE):
            for g, (first, width, axes) in enumerate(GROUPS):
                mix[g, i * TOK:(i + 1) * TOK, :] = jnp.where(
                    spread(near(axes[1], i), ranks[g]) == slot, 1.0, 0.0).astype(jnp.bfloat16)

    def gather(q, h):
        for i in (2, 1, 3, 0):
            for g, (first, width, axes) in enumerate(GROUPS):
                v = near(axes[1], i)
                cols = slice(0, width) if h is None else half(g, h)
                rows = dot(mix[g, i * TOK:(i + 1) * TOK, :], blocks[g][:, cols])
                rows = rows.astype(jnp.bfloat16).reshape(8, 16, cols.stop - cols.start)
                if i == 0:
                    hop2[g][q, v, :, :, cols] = rows
                else:
                    packed[g][q, pl.ds(v * 8, 8), :, cols] = rows
                    s2(g, q, i, cols).start()

    def whole_gather(q):
        @pl.when(q > 0)
        def _():
            choose(q)
            gather(q, None)

    def forward(q):
        for g in range(3):
            came(hop2[g].at[q, pl.ds(0, 3)], s2_recv.at[g, q])
            for i, d in PAIRS:
                s3(g, q, i, d).start()

    def expert(q):
        for g, (first, width, axes) in enumerate(GROUPS):
            came(arrived[g].at[q], s3_recv.at[g, q])
            for c in (0, 1):
                part = arrived[g][q, pl.ds(c * 4, 4)]
                if axes[0] == 2:
                    for y in range(4):
                        for z in range(4):
                            at_row = c * 256 + z * 64 + y * 16
                            stacked[at_row:at_row + 16, first:first + width] = part[y, z]
                else:
                    stacked[c * 256:(c + 1) * 256, first:first + width] = dot(
                        swap(g), part.reshape(256, width)).astype(jnp.bfloat16)

        def tile(n, carry):
            cols = pl.ds(pl.multiple_of(n * 256, 256), 256)
            gate = dot(stacked[...], gate_v[:, cols])
            up = dot(stacked[...], up_v[:, cols])
            hidden[:, cols] = (gate / (1.0 + jnp.exp(-gate)) * up).astype(jnp.bfloat16)
            return carry

        lax.fori_loop(0, HIDDEN // 256, tile, 0)
        for g, (first, width, axes) in enumerate(GROUPS):
            result = dot(hidden[...], down_v[:, first:first + width]).astype(jnp.bfloat16)
            went(packed[g].at[q, pl.ds(0, 24)], s2_send.at[g, q])
            for c in (0, 1):
                half = result[c * 256:(c + 1) * 256]
                if axes[0] == 2:
                    half = half.reshape(4, 4, 16, width)
                    for y in range(4):
                        for z in range(4):
                            packed[g][q, c * 16 + y * 4 + z] = half[z, y]
                else:
                    packed[g][q, pl.ds(c * 16, 16)] = dot(swap(g), half).astype(jnp.bfloat16).reshape(16, 16, width)
            for i, d in PAIRS:
                r3(g, q, i, d).start()

    def back(q):
        for g in range(3):
            came(back3[g].at[q], r3_recv.at[g, q])
        for h in (0, 1):
            for i in (2, 1, 3, 0):
                for g in range(3):
                    r2(g, q, i, h).start()

    def leave(g):
        first, width, axes = GROUPS[g]
        return pltpu.make_async_copy(
            blocks[g].at[own(g)], parts.at[3, :, first:first + width], out_sem.at[g])

    def combine(q):
        slot = slot_of[...] + (q * SLOTS).astype(jnp.float32)
        for g in range(3):
            for v in range(SIDE):
                mix[g, v * TOK:(v + 1) * TOK, :] = jnp.where(
                    spread(v, ranks[g]) == slot, spread(v, weights[g]), 0.0).astype(jnp.bfloat16)
        for h in (0, 1):
            for g, (first, width, axes) in enumerate(GROUPS):
                cols = half(g, h)
                came(back2[g].at[q, :, :, :, cols], r2_recv.at[g, q, h])
                total[g][:, cols] += dot_tn(
                    mix[g], back2[g][q, :, :, :, cols].reshape(SIDE * TOK, cols.stop - cols.start))

                @pl.when(q == ROUNDS - 1)
                def _():
                    if h == 0:
                        went(blocks[g].at[pl.ds(0, 3 * TOK)], s1_send.at[g])
                    blocks[g][:, cols] = total[g][:, cols].astype(jnp.bfloat16)
                    for i in (2, 1, 3):
                        r1(g, i, h).start()
                    if h == 1:
                        leave(g).start()

    def along_x():
        came(pieces.at[mine, pl.ds(0, 7)], t_recv.at[0])
        for i in (2, 1, 3):
            su(i).start()

    def across():
        came(pieces.at[pl.ds(0, 3)], u_recv.at[1])
        sv().start()

    def shares():
        came(pieces.at[pl.ds(0, 4)], u_recv.at[0])
        for r in range(8):
            for p in range(8):
                table[r * 256 + p * PIECE:r * 256 + (p + 1) * PIECE, :] = pieces[p, r]
        logits = dot(normed[...], table[...])
        eye = jnp.where(iota((TOK, TOK), 0) == iota((TOK, TOK), 1), 1.0, 0.0).astype(jnp.bfloat16)
        member = dot_nt(eye, members().astype(jnp.bfloat16))
        powers = jnp.where(member > 0.5, jnp.exp(logits), 0.0)
        share = (powers / jnp.sum(powers, axis=1, keepdims=True)).astype(jnp.bfloat16)
        for g, (first, width, axes) in enumerate(GROUPS):
            shares_out[g] = dot_nt(holder(g), share).astype(jnp.bfloat16)
            weights[g, :, own(g)] = shares_out[g, pl.ds(pl.multiple_of(at[axes[0]] * 32, 32), 32), :]
        for g in range(3):
            for i in (2, 1, 3):
                sp(g, i).start()

    def prepare():
        came(weights.at[:, :, pl.ds(0, 3 * TOK)], p_recv.at[0])
        for g in range(3):
            total[g][...] = jnp.zeros(total[g].shape, jnp.float32)

    came(ranks.at[:, :, pl.ds(0, 3 * TOK)], q_recv.at[0])
    choose(0)
    for h in (0, 1):
        for g in range(3):
            came(blocks[g].at[pl.ds(0, 3 * TOK), half(g, h)], s1_recv.at[g, h])
        gather(0, h)

    def step(k, carry):
        def stage(lag, run):
            @pl.when(jnp.logical_and(k >= lag, k < lag + ROUNDS))
            def _():
                run(k - lag)

        def once(when, run):
            @pl.when(k == when)
            def _():
                run()

        stage(0, whole_gather)
        once(0, along_x)
        once(1, across)
        stage(1, forward)
        once(2, shares)

        @pl.when(k == 2)
        def _():
            for load in loads:
                load.wait()

        stage(2, expert)
        stage(3, back)
        once(3, prepare)
        stage(4, combine)
        return carry

    lax.fori_loop(0, ROUNDS + 4, step, 0)

    for g, (first, width, axes) in enumerate(GROUPS):
        came(parts.at[pl.ds(0, 3), :, first:first + width], r1_recv.at[g])
    went(pieces.at[pl.ds(0, 4)], u_send.at[0])
    went(pieces.at[pl.ds(0, 3)], u_send.at[1])
    went(pieces.at[0, pl.ds(0, 7)], t_send.at[0])
    went(ranks.at[:, :, pl.ds(0, 3 * TOK)], q_send.at[0])
    went(weights.at[:, :, pl.ds(0, 3 * TOK)], p_send.at[0])
    for g in range(3):
        went(hop2[g].at[:, :, pl.ds(0, 7)], s3_send.at[g])
        went(hop2[g].at[:, :, pl.ds(0, 7)], r3_send.at[g])
        went(back3[g].at[:, pl.ds(0, 3)], r2_send.at[g])
        went(blocks[g].at[pl.ds(0, 3 * TOK)], r1_send.at[g])
        leave(g).wait()


def per_group(shape):
    return [pltpu.VMEM(shape(width), jnp.bfloat16) for _, width, _ in GROUPS]


def flat_kernel(*refs):
    args, rest = refs[:9], list(refs[9:])

    def take(n):
        head = rest[:n]
        del rest[:n]
        return head

    blocks = take(3)
    ranks, weights = take(2)
    packed, hop2, arrived, back3, back2, total = (take(3) for _ in range(6))
    kernel(*args, blocks, ranks, weights, packed, hop2, arrived, back3, back2, total, *rest)


def per_device(tokens, norm_gain, router, routes, placement, w_gate, w_up, w_down):
    dma = pltpu.SemaphoreType.DMA
    bf = jnp.bfloat16
    scratch = (
        per_group(lambda w: (SIDE * TOK, w))
        + [pltpu.VMEM((3, 32, SIDE * TOK), bf), pltpu.VMEM((3, 32, SIDE * TOK), bf)]
        + per_group(lambda w: (ROUNDS, 32, 16, w))
        + per_group(lambda w: (ROUNDS, 4, 8, 16, w))
        + per_group(lambda w: (ROUNDS, 8, 4, 16, w))
        + per_group(lambda w: (ROUNDS, 4, 8, 16, w))
        + per_group(lambda w: (ROUNDS, 4, 8, 16, w))
        + [pltpu.VMEM((SIDE * TOK, w), jnp.float32) for _, w, _ in GROUPS]
        + [
            pltpu.VMEM((WIDTH, HIDDEN), bf),
            pltpu.VMEM((WIDTH, HIDDEN), bf),
            pltpu.VMEM((HIDDEN, WIDTH), bf),
            pltpu.VMEM((TOK, WIDTH), bf),
            pltpu.VMEM((WIDTH, DEVICES), bf),
            pltpu.VMEM((8, 8, PIECE, DEVICES), bf),
            pltpu.VMEM((SIDE * TOK, WIDTH), bf),
            pltpu.VMEM((SIDE * TOK, HIDDEN), bf),
            pltpu.VMEM((TOK, SIDE * TOK), jnp.float32),
            pltpu.VMEM((3, SIDE * TOK, SIDE * TOK), bf),
            pltpu.VMEM((TOK, WIDTH), bf),
            pltpu.VMEM((1, WIDTH), jnp.float32),
            pltpu.VMEM((8, TOK), jnp.int32),
            pltpu.VMEM((1, DEVICES), jnp.int32),
            pltpu.VMEM((3, DEVICES, TOK), bf),
            pltpu.VMEM((3, DEVICES, TOK), bf),
            dma((3,)), dma((5,)), dma((3,)),
            dma((1,)), dma((1,)),
            dma((2,)), dma((2,)),
            dma((3,)), dma((3, 2)),
            dma((1,)), dma((1,)),
            dma((1,)), dma((1,)),
            dma((3, ROUNDS)), dma((3, ROUNDS)),
            dma((3,)), dma((3, ROUNDS)),
            dma((3,)), dma((3, ROUNDS)),
            dma((3,)), dma((3, ROUNDS, 2)),
            dma((3,)), dma((3,)),
        ]
    )
    whole = pl.BlockSpec(memory_space=pl.ANY)
    parts = pl.pallas_call(
        flat_kernel,
        name="moe",
        out_shape=jax.ShapeDtypeStruct((SIDE, TOK, WIDTH), bf),
        in_specs=[whole] * 8,
        out_specs=whole,
        scratch_shapes=scratch,
        compiler_params=pltpu.CompilerParams(
            collective_id=0, has_side_effects=True, vmem_limit_bytes=63 * 2**20
        ),
        cost_estimate=pl.CostEstimate(flops=15 * 10**9, bytes_accessed=11 * 10**6, transcendentals=10**6),
    )(tokens, norm_gain.reshape(1, WIDTH), router, routes.T, placement.reshape(1, DEVICES), w_gate, w_up, w_down)
    one, two, three, own = (parts[i].astype(jnp.float32) for i in range(SIDE))
    return (own + one + two + three).astype(bf)


def solution(mesh):
    placed = (
        P(("rep", "expert"), None),
        P(),
        P("rep", None),
        P(("rep", "expert"), None),
        P(),
        P(("rep", "expert"), None, None),
        P(("rep", "expert"), None, None),
        P(("rep", "expert"), None, None),
    )
    return jax.shard_map(
        per_device,
        mesh=mesh,
        in_specs=placed,
        out_specs=P(("rep", "expert"), None),
        check_vma=False,
    )
```

```python
import jax
import jax.numpy as jnp
from jax import lax
from jax.experimental import pallas as pl
from jax.experimental.pallas import tpu as pltpu
from jax.sharding import PartitionSpec as P

MESH = pl.DeviceIdType.MESH
TOK = 128
WIDTH = 2048
HIDDEN = 768
SIDE = 4
ROUNDS = 3
SLOTS = 4
DEVICES = 128
GROUPS = (
    (0, 768, (2, 0, 1)),
    (768, 640, (0, 1, 2)),
    (1408, 640, (1, 2, 0)),
)
NT = (((1,), (1,)), ((), ()))
PIECE = 32
HALF = 384


def iota(shape, dim):
    return lax.broadcasted_iota(jnp.int32, shape, dim)


def dot(a, b):
    return jnp.dot(a, b, preferred_element_type=jnp.float32)


def dot_nt(a, b):
    return lax.dot_general(a, b, NT, preferred_element_type=jnp.float32)


def kernel(
    tokens, gain, router, routes, placement, w_gate, w_up, w_down, own_part, low_part, high_part,
    blocks, ranks, weights, packed, hop2, arrived, back3, back2, passing, total,
    gate_v, up_v, down_v, normed, table, pieces, stacked, hidden, slot_of, mix,
    tokens_v, gain_v, routes_v, placement_v, ranks_out, shares_out,
    w_sem, in_sem, out_sem, t_send, t_recv, u_send, u_recv,
    s1_send, s1_recv, q_send, q_recv, p_send, p_recv, s2_send, s2_recv, s3_send, s3_recv, r3_send, r3_recv, r2_send, r2_recv, r1_send, r1_recv, f_recv,
):
    rep = lax.axis_index("rep")
    exp = lax.axis_index("expert")
    core = exp % 2
    at = (rep // 2, (rep % 2) * 2 + exp // 8, (exp // 2) % 4)

    def device(pos, c):
        z, y, x = pos
        return (z * 2 + y // 2, (y % 2) * 8 + x * 2 + c)

    def along(axis, value, c):
        pos = list(at)
        pos[axis] = value
        return device(pos, c)

    def near(axis, step):
        return (at[axis] + step) % SIDE

    def remote(src, dst, send, recv, dev):
        return pltpu.make_async_remote_copy(
            src_ref=src, dst_ref=dst, send_sem=send, recv_sem=recv,
            device_id=dev, device_id_type=MESH,
        )

    def came(ref, sem):
        remote(ref, ref, sem, sem, device(at, 1 - core)).wait_recv()

    def went(ref, sem):
        remote(ref, ref, sem, sem, device(at, 1 - core)).wait_send()

    barrier = pltpu.get_barrier_semaphore()
    greeted = [along(a, near(a, i), (core + d) % 2) for a in range(3) for i in (1, 2, 3) for d in (0, 1)]
    greeted.append(device(at, 1 - core))
    greeted += [device((near(0, i), near(1, 2), at[2]), core) for i in (1, 2, 3)]
    for dev in greeted:
        pl.semaphore_signal(barrier, inc=1, device_id=dev, device_id_type=MESH)

    mine = core * 4 + at[2]
    operands = [
        pltpu.make_async_copy(tokens, tokens_v, in_sem.at[0]),
        pltpu.make_async_copy(gain, gain_v, in_sem.at[1]),
        pltpu.make_async_copy(routes, routes_v, in_sem.at[2]),
        pltpu.make_async_copy(placement, placement_v, in_sem.at[3]),
        pltpu.make_async_copy(
            router.at[pl.ds(pl.multiple_of(mine * PIECE, PIECE), PIECE)], pieces.at[mine, rep], in_sem.at[4]),
    ]
    for load in operands:
        load.start()
    loads = [
        pltpu.make_async_copy(w_gate.at[0], gate_v, w_sem.at[0]),
        pltpu.make_async_copy(w_up.at[0], up_v, w_sem.at[1]),
        pltpu.make_async_copy(w_down.at[0], down_v, w_sem.at[2]),
    ]
    for load in loads:
        load.start()

    operands[0].wait()
    operands[1].wait()
    values = tokens_v[...].astype(jnp.float32)
    scale = lax.rsqrt(jnp.mean(values * values, axis=-1, keepdims=True) + 1e-06)
    normed[...] = (values * scale * gain_v[...]).astype(jnp.bfloat16)
    for g, (first, width, axes) in enumerate(GROUPS):
        blocks[g][pl.ds(pl.multiple_of(at[axes[0]] * TOK, TOK), TOK), :] = normed[:, first:first + width]

    def holder(g):
        a1, a2, a3 = GROUPS[g][2]
        r = iota((DEVICES, DEVICES), 0)
        pos = [None, None, None]
        pos[a1] = r // 32
        pos[a2] = (r // 8) % 4
        pos[a3] = (r // 2) % 4
        wanted = pos[0] * 32 + pos[1] * 8 + pos[2] * 2 + r % 2
        return jnp.where(placement_v[...] == wanted, 1.0, 0.0).astype(jnp.bfloat16)

    def members():
        found = jnp.zeros((DEVICES, TOK), jnp.float32)
        rows = iota((DEVICES, TOK), 0)
        for k in range(8):
            found = found + jnp.where(routes_v[k:k + 1, :] == rows, 1.0, 0.0)
        return found

    operands[2].wait()
    operands[3].wait()
    member = members()
    before = jnp.where(iota((TOK, TOK), 0) < iota((TOK, TOK), 1), 1.0, 0.0).astype(jnp.bfloat16)
    rank = jnp.where(member > 0.5, dot(member.astype(jnp.bfloat16), before), -1.0).astype(jnp.bfloat16)
    for g, (first, width, axes) in enumerate(GROUPS):
        ranks_out[g] = dot(holder(g), rank).astype(jnp.bfloat16)
        ranks[g, :, pl.ds(pl.multiple_of(at[axes[0]] * TOK, TOK), TOK)] = ranks_out[
            g, pl.ds(pl.multiple_of(at[axes[0]] * 32, 32), 32), :]
    operands[4].wait()

    pl.semaphore_wait(barrier, len(greeted))

    def block(g, position):
        return pl.ds(pl.multiple_of(position * TOK, TOK), TOK)

    def own(g):
        return block(g, at[GROUPS[g][2][0]])

    def half(g, h):
        return slice(0, HALF) if h == 0 else slice(HALF, GROUPS[g][1])

    def s1(g, i, h):
        a = GROUPS[g][2][0]
        mine = blocks[g].at[own(g), half(g, h)]
        return remote(mine, mine, s1_send.at[g], s1_recv.at[g, h],
                      along(a, near(a, i), core))

    def sq(g, i):
        a = GROUPS[g][2][0]
        v = near(a, i)
        return remote(ranks_out.at[g, pl.ds(pl.multiple_of(v * 32, 32), 32)], ranks.at[g, :, own(g)],
                      q_send.at[0], q_recv.at[0], along(a, v, core))

    def sp(g, i):
        a = GROUPS[g][2][0]
        v = near(a, i)
        return remote(shares_out.at[g, pl.ds(pl.multiple_of(v * 32, 32), 32)], weights.at[g, :, own(g)],
                      p_send.at[0], p_recv.at[0], along(a, v, core))

    def st(i):
        return remote(pieces.at[mine, rep], pieces.at[mine, rep],
                      t_send.at[0], t_recv.at[0], ((rep + i) % 8, exp))

    def su(i):
        return remote(pieces.at[mine], pieces.at[mine],
                      u_send.at[1], u_recv.at[1], along(2, near(2, i), core))

    def sv():
        return remote(pieces.at[pl.ds(core * 4, 4)], pieces.at[pl.ds(core * 4, 4)],
                      u_send.at[0], u_recv.at[0], device(at, 1 - core))

    for i in (2, 1, 3):
        for g in range(3):
            s1(g, i, 0).start()
    for g in range(3):
        for i in (2, 1, 3):
            sq(g, i).start()
    for i in (2, 1, 3):
        for g in range(3):
            s1(g, i, 1).start()
    for i in range(1, 8):
        st(i).start()

    row = iota((TOK, SIDE * TOK), 0)
    col = iota((TOK, SIDE * TOK), 1)
    slot_of[...] = jnp.where((row // 4) % 4 == col // TOK, row % 4, 1000).astype(jnp.float32)

    def spread(v, plane):
        r = iota((TOK, 32), 0)
        pick = jnp.where(iota((TOK, 32), 1) == v * 8 + r // 16, 1.0, 0.0).astype(jnp.bfloat16)
        return dot(pick, plane)

    def swap(g):
        r = iota((256, 256), 0)
        c = iota((256, 256), 1)
        a, b, d, s = r // 64, (r // 16) % 4, (r // 4) % 4, r % 4
        if GROUPS[g][2][0] == 0:
            wanted = d * 64 + b * 16 + a * 4 + s
        else:
            wanted = a * 64 + d * 16 + b * 4 + s
        return jnp.where(c == wanted, 1.0, 0.0).astype(jnp.bfloat16)

    def s2(g, q, i, cols):
        a = GROUPS[g][2][1]
        v = near(a, i)
        return remote(packed[g].at[q, pl.ds(v * 8, 8), :, cols], hop2[g].at[q, at[a], :, :, cols],
                      s2_send.at[g, q], s2_recv.at[g, q], along(a, v, core))

    def s3(g, q, i, d):
        a = GROUPS[g][2][2]
        u, c = near(a, i), (core + d) % 2
        src = hop2[g].at[q, :, u * 2 + c]
        dst = arrived[g].at[q, core * 4 + at[a]]
        if i == 0 and d == 0:
            return pltpu.make_async_copy(src, dst, s3_recv.at[g, q])
        return remote(src, dst, s3_send.at[g], s3_recv.at[g, q], along(a, u, c))

    def r3(g, q, i, d):
        a = GROUPS[g][2][2]
        u, c = near(a, i), (core + d) % 2
        src = packed[g].at[q, pl.ds((c * 4 + u) * 4, 4)]
        dst = back3[g].at[q, :, at[a] * 2 + core]
        if i == 0 and d == 0:
            return pltpu.make_async_copy(src, dst, r3_recv.at[g, q])
        return remote(src, dst, r3_send.at[g], r3_recv.at[g, q], along(a, u, c))

    def r2(g, q, i, h):
        a = GROUPS[g][2][1]
        v = near(a, i)
        cols = half(g, h)
        src, dst = back3[g].at[q, v, :, :, cols], back2[g].at[q, at[a], :, :, cols]
        if i == 0:
            return pltpu.make_async_copy(src, dst, r2_recv.at[g, q, h])
        return remote(src, dst, r2_send.at[g], r2_recv.at[g, q, h], along(a, v, core))

    def far(g, h):
        a = GROUPS[g][2][0]
        cols = half(g, h)
        return remote(blocks[g].at[block(g, near(a, 2)), cols], passing[g].at[:, cols],
                      r1_send.at[g], f_recv.at[g, h], along(a, near(a, 1 if h == 0 else 3), core))

    def home(g, h, up):
        first, width, axes = GROUPS[g]
        a = axes[0]
        cols = half(g, h)
        v = near(a, 1 if up else 3)
        part = low_part if up else high_part
        return remote(blocks[g].at[block(g, v), cols], part.at[:, first + cols.start:first + cols.stop],
                      r1_send.at[g], r1_recv.at[g], along(a, v, core))

    PAIRS = [(i, d) for i in (2, 1, 3, 0) for d in (0, 1)]

    def choose(q):
        slot = slot_of[...] + jnp.asarray(q * SLOTS, jnp.float32)
        for i in range(SIDE):
            for g, (first, width, axes) in enumerate(GROUPS):
                mix[g, i * TOK:(i + 1) * TOK, :] = jnp.where(
                    spread(near(axes[1], i), ranks[g]) == slot, 1.0, 0.0).astype(jnp.bfloat16)

    def gather(q, h):
        for i in (2, 1, 3, 0):
            for g, (first, width, axes) in enumerate(GROUPS):
                v = near(axes[1], i)
                cols = slice(0, width) if h is None else half(g, h)
                rows = dot(mix[g, i * TOK:(i + 1) * TOK, :], blocks[g][:, cols])
                rows = rows.astype(jnp.bfloat16).reshape(8, 16, cols.stop - cols.start)
                if i == 0:
                    hop2[g][q, v, :, :, cols] = rows
                else:
                    packed[g][q, pl.ds(v * 8, 8), :, cols] = rows
                    s2(g, q, i, cols).start()

    def whole_gather(q):
        @pl.when(q > 0)
        def _():
            choose(q)
            gather(q, None)

    def forward(q):
        for g in range(3):
            came(hop2[g].at[q, pl.ds(0, 3)], s2_recv.at[g, q])
            for i, d in PAIRS:
                s3(g, q, i, d).start()

    def expert(q):
        for g, (first, width, axes) in enumerate(GROUPS):
            came(arrived[g].at[q], s3_recv.at[g, q])
            for c in (0, 1):
                part = arrived[g][q, pl.ds(c * 4, 4)]
                if axes[0] == 2:
                    for y in range(4):
                        for z in range(4):
                            at_row = c * 256 + z * 64 + y * 16
                            stacked[at_row:at_row + 16, first:first + width] = part[y, z]
                else:
                    stacked[c * 256:(c + 1) * 256, first:first + width] = dot(
                        swap(g), part.reshape(256, width)).astype(jnp.bfloat16)

        def tile(n, carry):
            cols = pl.ds(pl.multiple_of(n * 256, 256), 256)
            gate = dot(stacked[...], gate_v[:, cols])
            up = dot(stacked[...], up_v[:, cols])
            hidden[:, cols] = (gate / (1.0 + jnp.exp(-gate)) * up).astype(jnp.bfloat16)
            return carry

        lax.fori_loop(0, HIDDEN // 256, tile, 0)
        for g, (first, width, axes) in enumerate(GROUPS):
            result = dot(hidden[...], down_v[:, first:first + width]).astype(jnp.bfloat16)
            went(packed[g].at[q, pl.ds(0, 24)], s2_send.at[g, q])
            for c in (0, 1):
                half = result[c * 256:(c + 1) * 256]
                if axes[0] == 2:
                    half = half.reshape(4, 4, 16, width)
                    for y in range(4):
                        for z in range(4):
                            packed[g][q, c * 16 + y * 4 + z] = half[z, y]
                else:
                    packed[g][q, pl.ds(c * 16, 16)] = dot(swap(g), half).astype(jnp.bfloat16).reshape(16, 16, width)
            for i, d in PAIRS:
                r3(g, q, i, d).start()

    def back(q):
        for g in range(3):
            came(back3[g].at[q], r3_recv.at[g, q])
        for h in (0, 1):
            for i in (2, 1, 3, 0):
                for g in range(3):
                    r2(g, q, i, h).start()

    def leave(g):
        first, width, axes = GROUPS[g]
        return pltpu.make_async_copy(
            blocks[g].at[own(g)], own_part.at[:, first:first + width], out_sem.at[g])

    def combine(q):
        slot = slot_of[...] + (q * SLOTS).astype(jnp.float32)
        for g in range(3):
            for v in range(SIDE):
                mix[g, :, v * TOK:(v + 1) * TOK] = jnp.transpose(jnp.where(
                    spread(v, ranks[g]) == slot, spread(v, weights[g]), 0.0)).astype(jnp.bfloat16)
        for h in (0, 1):
            for g, (first, width, axes) in enumerate(GROUPS):
                cols = half(g, h)
                came(back2[g].at[q, :, :, :, cols], r2_recv.at[g, q, h])
                total[g][:, cols] += dot(
                    mix[g], back2[g][q, :, :, :, cols].reshape(SIDE * TOK, cols.stop - cols.start))

                @pl.when(q == ROUNDS - 1)
                def _():
                    if h == 0:
                        went(blocks[g].at[pl.ds(0, 3 * TOK)], s1_send.at[g])
                    blocks[g][:, cols] = total[g][:, cols].astype(jnp.bfloat16)
                    far(g, h).start()
                    home(g, h, h == 1).start()
                    if h == 1:
                        leave(g).start()

    def along_x():
        came(pieces.at[mine, pl.ds(0, 7)], t_recv.at[0])
        for i in (2, 1, 3):
            su(i).start()

    def across():
        came(pieces.at[pl.ds(0, 3)], u_recv.at[1])
        sv().start()

    def shares():
        came(pieces.at[pl.ds(0, 4)], u_recv.at[0])
        for r in range(8):
            for p in range(8):
                table[r * 256 + p * PIECE:r * 256 + (p + 1) * PIECE, :] = pieces[p, r]
        logits = dot(normed[...], table[...])
        eye = jnp.where(iota((TOK, TOK), 0) == iota((TOK, TOK), 1), 1.0, 0.0).astype(jnp.bfloat16)
        member = dot_nt(eye, members().astype(jnp.bfloat16))
        powers = jnp.where(member > 0.5, jnp.exp(logits), 0.0)
        share = (powers / jnp.sum(powers, axis=1, keepdims=True)).astype(jnp.bfloat16)
        for g, (first, width, axes) in enumerate(GROUPS):
            shares_out[g] = dot_nt(holder(g), share).astype(jnp.bfloat16)
            weights[g, :, own(g)] = shares_out[g, pl.ds(pl.multiple_of(at[axes[0]] * 32, 32), 32), :]
        for g in range(3):
            for i in (2, 1, 3):
                sp(g, i).start()

    def prepare():
        came(weights.at[:, :, pl.ds(0, 3 * TOK)], p_recv.at[0])
        for g in range(3):
            total[g][...] = jnp.zeros(total[g].shape, jnp.float32)

    came(ranks.at[:, :, pl.ds(0, 3 * TOK)], q_recv.at[0])
    choose(0)
    for h in (0, 1):
        for g in range(3):
            came(blocks[g].at[pl.ds(0, 3 * TOK), half(g, h)], s1_recv.at[g, h])
        gather(0, h)

    def step(k, carry):
        def stage(lag, run):
            @pl.when(jnp.logical_and(k >= lag, k < lag + ROUNDS))
            def _():
                run(k - lag)

        def once(when, run):
            @pl.when(k == when)
            def _():
                run()

        stage(0, whole_gather)
        once(0, along_x)
        once(1, across)
        stage(1, forward)
        once(2, shares)

        @pl.when(k == 2)
        def _():
            for load in loads:
                load.wait()

        stage(2, expert)
        stage(3, back)
        once(3, prepare)
        stage(4, combine)
        return carry

    lax.fori_loop(0, ROUNDS + 4, step, 0)

    for h in (0, 1):
        for g, (first, width, axes) in enumerate(GROUPS):
            cols = half(g, h)
            came(passing[g].at[:, cols], f_recv.at[g, h])
            rows = block(g, near(axes[0], 1 if h == 0 else 3))
            both = total[g][rows, cols] + passing[g][:, cols].astype(jnp.float32)
            blocks[g][rows, cols] = both.astype(jnp.bfloat16)
            home(g, h, h == 0).start()
    for g in range(3):
        came(blocks[g].at[pl.ds(0, 2 * TOK)], r1_recv.at[g])
    went(pieces.at[pl.ds(0, 4)], u_send.at[0])
    went(pieces.at[pl.ds(0, 3)], u_send.at[1])
    went(pieces.at[0, pl.ds(0, 7)], t_send.at[0])
    went(ranks.at[:, :, pl.ds(0, 3 * TOK)], q_send.at[0])
    went(weights.at[:, :, pl.ds(0, 3 * TOK)], p_send.at[0])
    for g in range(3):
        went(hop2[g].at[:, :, pl.ds(0, 7)], s3_send.at[g])
        went(hop2[g].at[:, :, pl.ds(0, 7)], r3_send.at[g])
        went(back3[g].at[:, pl.ds(0, 3)], r2_send.at[g])
        went(blocks[g].at[pl.ds(0, 3 * TOK)], r1_send.at[g])
        leave(g).wait()


def per_group(shape):
    return [pltpu.VMEM(shape(width), jnp.bfloat16) for _, width, _ in GROUPS]


def flat_kernel(*refs):
    args, rest = refs[:11], list(refs[11:])

    def take(n):
        head = rest[:n]
        del rest[:n]
        return head

    blocks = take(3)
    ranks, weights = take(2)
    packed, hop2, arrived, back3, back2, passing, total = (take(3) for _ in range(7))
    kernel(*args, blocks, ranks, weights, packed, hop2, arrived, back3, back2, passing, total, *rest)


def per_device(tokens, norm_gain, router, routes, placement, w_gate, w_up, w_down):
    dma = pltpu.SemaphoreType.DMA
    bf = jnp.bfloat16
    scratch = (
        per_group(lambda w: (SIDE * TOK, w))
        + [pltpu.VMEM((3, 32, SIDE * TOK), bf), pltpu.VMEM((3, 32, SIDE * TOK), bf)]
        + per_group(lambda w: (ROUNDS, 32, 16, w))
        + per_group(lambda w: (ROUNDS, 4, 8, 16, w))
        + per_group(lambda w: (ROUNDS, 8, 4, 16, w))
        + per_group(lambda w: (ROUNDS, 4, 8, 16, w))
        + per_group(lambda w: (ROUNDS, 4, 8, 16, w))
        + per_group(lambda w: (TOK, w))
        + [pltpu.VMEM((SIDE * TOK, w), jnp.float32) for _, w, _ in GROUPS]
        + [
            pltpu.VMEM((WIDTH, HIDDEN), bf),
            pltpu.VMEM((WIDTH, HIDDEN), bf),
            pltpu.VMEM((HIDDEN, WIDTH), bf),
            pltpu.VMEM((TOK, WIDTH), bf),
            pltpu.VMEM((WIDTH, DEVICES), bf),
            pltpu.VMEM((8, 8, PIECE, DEVICES), bf),
            pltpu.VMEM((SIDE * TOK, WIDTH), bf),
            pltpu.VMEM((SIDE * TOK, HIDDEN), bf),
            pltpu.VMEM((TOK, SIDE * TOK), jnp.float32),
            pltpu.VMEM((3, SIDE * TOK, SIDE * TOK), bf),
            pltpu.VMEM((TOK, WIDTH), bf),
            pltpu.VMEM((1, WIDTH), jnp.float32),
            pltpu.VMEM((8, TOK), jnp.int32),
            pltpu.VMEM((1, DEVICES), jnp.int32),
            pltpu.VMEM((3, DEVICES, TOK), bf),
            pltpu.VMEM((3, DEVICES, TOK), bf),
            dma((3,)), dma((5,)), dma((3,)),
            dma((1,)), dma((1,)),
            dma((2,)), dma((2,)),
            dma((3,)), dma((3, 2)),
            dma((1,)), dma((1,)),
            dma((1,)), dma((1,)),
            dma((3, ROUNDS)), dma((3, ROUNDS)),
            dma((3,)), dma((3, ROUNDS)),
            dma((3,)), dma((3, ROUNDS)),
            dma((3,)), dma((3, ROUNDS, 2)),
            dma((3,)), dma((3,)), dma((3, 2)),
        ]
    )
    whole = pl.BlockSpec(memory_space=pl.ANY)
    own, low, high = pl.pallas_call(
        flat_kernel,
        name="moe",
        out_shape=[jax.ShapeDtypeStruct((TOK, WIDTH), bf)] * 3,
        in_specs=[whole] * 8,
        out_specs=[whole] * 3,
        scratch_shapes=scratch,
        compiler_params=pltpu.CompilerParams(
            collective_id=0, has_side_effects=True, vmem_limit_bytes=63 * 2**20
        ),
        cost_estimate=pl.CostEstimate(flops=15 * 10**9, bytes_accessed=11 * 10**6, transcendentals=10**6),
    )(tokens, norm_gain.reshape(1, WIDTH), router, routes.T, placement.reshape(1, DEVICES), w_gate, w_up, w_down)
    return (own.astype(jnp.float32) + low.astype(jnp.float32) + high.astype(jnp.float32)).astype(bf)


def solution(mesh):
    placed = (
        P(("rep", "expert"), None),
        P(),
        P("rep", None),
        P(("rep", "expert"), None),
        P(),
        P(("rep", "expert"), None, None),
        P(("rep", "expert"), None, None),
        P(("rep", "expert"), None, None),
    )
    return jax.shard_map(
        per_device,
        mesh=mesh,
        in_specs=placed,
        out_specs=P(("rep", "expert"), None),
        check_vma=False,
    )
```

```python
import jax
import jax.numpy as jnp
from jax import lax
from jax.experimental import pallas as pl
from jax.experimental.pallas import tpu as pltpu
from jax.sharding import PartitionSpec as P

MESH = pl.DeviceIdType.MESH
TOK = 128
WIDTH = 2048
HIDDEN = 768
SIDE = 4
ROUNDS = 3
SLOTS = 4
DEVICES = 128
GROUPS = (
    (0, 768, (2, 0, 1)),
    (768, 640, (0, 1, 2)),
    (1408, 640, (1, 2, 0)),
)
NT = (((1,), (1,)), ((), ()))
PIECE = 32
HALF = 384


def iota(shape, dim):
    return lax.broadcasted_iota(jnp.int32, shape, dim)


def dot(a, b):
    return jnp.dot(a, b, preferred_element_type=jnp.float32)


def dot_nt(a, b):
    return lax.dot_general(a, b, NT, preferred_element_type=jnp.float32)


def kernel(
    tokens, gain, router, routes, placement, w_gate, w_up, w_down, own_part, low_part, high_part,
    blocks, ranks, weights, packed, hop2, arrived, back3, back2, passing, total,
    gate_v, up_v, down_v, normed, table, pieces, stacked, hidden, slot_of, mix,
    tokens_v, gain_v, routes_v, placement_v, ranks_out, shares_out,
    w_sem, in_sem, out_sem, t_send, t_recv, u_send, u_recv,
    s1_send, s1_recv, q_send, q_recv, p_send, p_recv, s2_send, s2_recv, s3_send, s3_recv, r3_send, r3_recv, r2_send, r2_recv, r1_send, r1_recv, f_recv,
):
    rep = lax.axis_index("rep")
    exp = lax.axis_index("expert")
    core = exp % 2
    at = (rep // 2, (rep % 2) * 2 + exp // 8, (exp // 2) % 4)

    def device(pos, c):
        z, y, x = pos
        return (z * 2 + y // 2, (y % 2) * 8 + x * 2 + c)

    def along(axis, value, c):
        pos = list(at)
        pos[axis] = value
        return device(pos, c)

    def near(axis, step):
        return (at[axis] + step) % SIDE

    def remote(src, dst, send, recv, dev):
        return pltpu.make_async_remote_copy(
            src_ref=src, dst_ref=dst, send_sem=send, recv_sem=recv,
            device_id=dev, device_id_type=MESH,
        )

    def came(ref, sem):
        remote(ref, ref, sem, sem, device(at, 1 - core)).wait_recv()

    def went(ref, sem):
        remote(ref, ref, sem, sem, device(at, 1 - core)).wait_send()

    barrier = pltpu.get_barrier_semaphore()
    greeted = [along(a, near(a, i), (core + d) % 2) for a in range(3) for i in (1, 2, 3) for d in (0, 1)]
    greeted.append(device(at, 1 - core))
    greeted += [device((near(0, i), near(1, 2), at[2]), core) for i in (1, 2, 3)]
    for dev in greeted:
        pl.semaphore_signal(barrier, inc=1, device_id=dev, device_id_type=MESH)

    mine = core * 4 + at[2]
    operands = [
        pltpu.make_async_copy(tokens, tokens_v, in_sem.at[0]),
        pltpu.make_async_copy(gain, gain_v, in_sem.at[1]),
        pltpu.make_async_copy(routes, routes_v, in_sem.at[2]),
        pltpu.make_async_copy(placement, placement_v, in_sem.at[3]),
        pltpu.make_async_copy(
            router.at[pl.ds(pl.multiple_of(mine * PIECE, PIECE), PIECE)], pieces.at[mine, rep], in_sem.at[4]),
    ]
    for load in operands:
        load.start()
    loads = [
        pltpu.make_async_copy(w_gate.at[0], gate_v, w_sem.at[0]),
        pltpu.make_async_copy(w_up.at[0], up_v, w_sem.at[1]),
        pltpu.make_async_copy(w_down.at[0], down_v, w_sem.at[2]),
    ]
    for load in loads:
        load.start()

    operands[0].wait()
    operands[1].wait()
    values = tokens_v[...].astype(jnp.float32)
    scale = lax.rsqrt(jnp.mean(values * values, axis=-1, keepdims=True) + 1e-06)
    normed[...] = (values * scale * gain_v[...]).astype(jnp.bfloat16)
    for g, (first, width, axes) in enumerate(GROUPS):
        blocks[g][pl.ds(pl.multiple_of(at[axes[0]] * TOK, TOK), TOK), :] = normed[:, first:first + width]

    def holder(g):
        a1, a2, a3 = GROUPS[g][2]
        r = iota((DEVICES, DEVICES), 0)
        pos = [None, None, None]
        pos[a1] = r // 32
        pos[a2] = (r // 8) % 4
        pos[a3] = (r // 2) % 4
        wanted = pos[0] * 32 + pos[1] * 8 + pos[2] * 2 + r % 2
        return jnp.where(placement_v[...] == wanted, 1.0, 0.0).astype(jnp.bfloat16)

    def members():
        found = jnp.zeros((DEVICES, TOK), jnp.float32)
        rows = iota((DEVICES, TOK), 0)
        for k in range(8):
            found = found + jnp.where(routes_v[k:k + 1, :] == rows, 1.0, 0.0)
        return found

    operands[2].wait()
    operands[3].wait()
    member = members()
    before = jnp.where(iota((TOK, TOK), 0) < iota((TOK, TOK), 1), 1.0, 0.0).astype(jnp.bfloat16)
    rank = jnp.where(member > 0.5, dot(member.astype(jnp.bfloat16), before), -1.0).astype(jnp.bfloat16)
    for g, (first, width, axes) in enumerate(GROUPS):
        ranks_out[g] = dot(holder(g), rank).astype(jnp.bfloat16)
        ranks[g, :, pl.ds(pl.multiple_of(at[axes[0]] * TOK, TOK), TOK)] = ranks_out[
            g, pl.ds(pl.multiple_of(at[axes[0]] * 32, 32), 32), :]
    operands[4].wait()

    pl.semaphore_wait(barrier, len(greeted))

    def block(g, position):
        return pl.ds(pl.multiple_of(position * TOK, TOK), TOK)

    def own(g):
        return block(g, at[GROUPS[g][2][0]])

    def half(g, h):
        return slice(0, HALF) if h == 0 else slice(HALF, GROUPS[g][1])

    def s1(g, i, h):
        a = GROUPS[g][2][0]
        mine = blocks[g].at[own(g), half(g, h)]
        return remote(mine, mine, s1_send.at[g], s1_recv.at[h],
                      along(a, near(a, i), core))

    def sq(g, i):
        a = GROUPS[g][2][0]
        v = near(a, i)
        return remote(ranks_out.at[g, pl.ds(pl.multiple_of(v * 32, 32), 32)], ranks.at[g, :, own(g)],
                      q_send.at[0], q_recv.at[0], along(a, v, core))

    def sp(g, i):
        a = GROUPS[g][2][0]
        v = near(a, i)
        return remote(shares_out.at[g, pl.ds(pl.multiple_of(v * 32, 32), 32)], weights.at[g, :, own(g)],
                      p_send.at[0], p_recv.at[0], along(a, v, core))

    def st(i):
        return remote(pieces.at[mine, rep], pieces.at[mine, rep],
                      t_send.at[0], t_recv.at[0], ((rep + i) % 8, exp))

    def su(i):
        return remote(pieces.at[mine], pieces.at[mine],
                      u_send.at[1], u_recv.at[1], along(2, near(2, i), core))

    def sv():
        return remote(pieces.at[pl.ds(core * 4, 4)], pieces.at[pl.ds(core * 4, 4)],
                      u_send.at[0], u_recv.at[0], device(at, 1 - core))

    for i in (2, 1, 3):
        for g in range(3):
            s1(g, i, 0).start()
    for g in range(3):
        for i in (2, 1, 3):
            sq(g, i).start()
    for i in (2, 1, 3):
        for g in range(3):
            s1(g, i, 1).start()
    for i in range(1, 8):
        st(i).start()

    row = iota((TOK, SIDE * TOK), 0)
    col = iota((TOK, SIDE * TOK), 1)
    slot_of[...] = jnp.where((row // 4) % 4 == col // TOK, row % 4, 1000).astype(jnp.float32)

    def spread(v, plane):
        r = iota((TOK, 32), 0)
        pick = jnp.where(iota((TOK, 32), 1) == v * 8 + r // 16, 1.0, 0.0).astype(jnp.bfloat16)
        return dot(pick, plane)

    def swap(g):
        r = iota((256, 256), 0)
        c = iota((256, 256), 1)
        a, b, d, s = r // 64, (r // 16) % 4, (r // 4) % 4, r % 4
        if GROUPS[g][2][0] == 0:
            wanted = d * 64 + b * 16 + a * 4 + s
        else:
            wanted = a * 64 + d * 16 + b * 4 + s
        return jnp.where(c == wanted, 1.0, 0.0).astype(jnp.bfloat16)

    def s2(g, q, i, cols):
        a = GROUPS[g][2][1]
        v = near(a, i)
        return remote(packed[g].at[q, pl.ds(v * 8, 8), :, cols], hop2[g].at[q, at[a], :, :, cols],
                      s2_send.at[q], s2_recv.at[g, q], along(a, v, core))

    def s3(g, q, i, d):
        a = GROUPS[g][2][2]
        u, c = near(a, i), (core + d) % 2
        src = hop2[g].at[q, :, u * 2 + c]
        dst = arrived[g].at[q, core * 4 + at[a]]
        if i == 0 and d == 0:
            return pltpu.make_async_copy(src, dst, s3_recv.at[q])
        return remote(src, dst, s3_send.at[g], s3_recv.at[q], along(a, u, c))

    def r3(g, q, i, d):
        a = GROUPS[g][2][2]
        u, c = near(a, i), (core + d) % 2
        src = packed[g].at[q, pl.ds((c * 4 + u) * 4, 4)]
        dst = back3[g].at[q, :, at[a] * 2 + core]
        if i == 0 and d == 0:
            return pltpu.make_async_copy(src, dst, r3_recv.at[q])
        return remote(src, dst, r3_send.at[g], r3_recv.at[q], along(a, u, c))

    def r2(g, q, i, h):
        a = GROUPS[g][2][1]
        v = near(a, i)
        cols = half(g, h)
        src, dst = back3[g].at[q, v, :, :, cols], back2[g].at[q, at[a], :, :, cols]
        if i == 0:
            return pltpu.make_async_copy(src, dst, r2_recv.at[g, q, h])
        return remote(src, dst, r2_send.at[g], r2_recv.at[g, q, h], along(a, v, core))

    def far(g, h):
        a = GROUPS[g][2][0]
        cols = half(g, h)
        return remote(blocks[g].at[block(g, near(a, 2)), cols], passing[g].at[:, cols],
                      r1_send.at[g], f_recv.at[g, h], along(a, near(a, 1 if h == 0 else 3), core))

    def home(g, h, up):
        first, width, axes = GROUPS[g]
        a = axes[0]
        cols = half(g, h)
        v = near(a, 1 if up else 3)
        part = low_part if up else high_part
        return remote(blocks[g].at[block(g, v), cols], part.at[:, first + cols.start:first + cols.stop],
                      r1_send.at[g], r1_recv.at[g], along(a, v, core))

    PAIRS = [(i, d) for i in (2, 1, 3, 0) for d in (0, 1)]

    def choose(q):
        slot = slot_of[...] + jnp.asarray(q * SLOTS, jnp.float32)
        for i in range(SIDE):
            for g, (first, width, axes) in enumerate(GROUPS):
                mix[g, i * TOK:(i + 1) * TOK, :] = jnp.where(
                    spread(near(axes[1], i), ranks[g]) == slot, 1.0, 0.0).astype(jnp.bfloat16)

    def gather(q, h):
        for i in (2, 1, 3, 0):
            for g, (first, width, axes) in enumerate(GROUPS):
                v = near(axes[1], i)
                cols = slice(0, width) if h is None else half(g, h)
                rows = dot(mix[g, i * TOK:(i + 1) * TOK, :], blocks[g][:, cols])
                rows = rows.astype(jnp.bfloat16).reshape(8, 16, cols.stop - cols.start)
                if i == 0:
                    hop2[g][q, v, :, :, cols] = rows
                else:
                    packed[g][q, pl.ds(v * 8, 8), :, cols] = rows
                    s2(g, q, i, cols).start()

    def whole_gather(q):
        @pl.when(q > 0)
        def _():
            choose(q)
            gather(q, None)

    def forward(q):
        for g in range(3):
            came(hop2[g].at[q, pl.ds(0, 3)], s2_recv.at[g, q])
            for i, d in PAIRS:
                s3(g, q, i, d).start()

    def expert(q):
        for g, (first, width, axes) in enumerate(GROUPS):
            if g == 0:
                came(stacked, s3_recv.at[q])
            for c in (0, 1):
                part = arrived[g][q, pl.ds(c * 4, 4)]
                if axes[0] == 2:
                    for y in range(4):
                        for z in range(4):
                            at_row = c * 256 + z * 64 + y * 16
                            stacked[at_row:at_row + 16, first:first + width] = part[y, z]
                else:
                    stacked[c * 256:(c + 1) * 256, first:first + width] = dot(
                        swap(g), part.reshape(256, width)).astype(jnp.bfloat16)

        def tile(n, carry):
            cols = pl.ds(pl.multiple_of(n * 256, 256), 256)
            gate = dot(stacked[...], gate_v[:, cols])
            up = dot(stacked[...], up_v[:, cols])
            hidden[:, cols] = (gate / (1.0 + jnp.exp(-gate)) * up).astype(jnp.bfloat16)
            return carry

        lax.fori_loop(0, HIDDEN // 256, tile, 0)
        for g, (first, width, axes) in enumerate(GROUPS):
            result = dot(hidden[...], down_v[:, first:first + width]).astype(jnp.bfloat16)
            if g == 0:
                went(stacked.at[pl.ds(0, 3 * TOK)], s2_send.at[q])
            for c in (0, 1):
                half = result[c * 256:(c + 1) * 256]
                if axes[0] == 2:
                    half = half.reshape(4, 4, 16, width)
                    for y in range(4):
                        for z in range(4):
                            packed[g][q, c * 16 + y * 4 + z] = half[z, y]
                else:
                    packed[g][q, pl.ds(c * 16, 16)] = dot(swap(g), half).astype(jnp.bfloat16).reshape(16, 16, width)
            for i, d in PAIRS:
                r3(g, q, i, d).start()

    def back(q):
        came(stacked, r3_recv.at[q])
        for h in (0, 1):
            for i in (2, 1, 3, 0):
                for g in range(3):
                    r2(g, q, i, h).start()

    def leave(g):
        first, width, axes = GROUPS[g]
        return pltpu.make_async_copy(
            blocks[g].at[own(g)], own_part.at[:, first:first + width], out_sem.at[g])

    def combine(q):
        slot = slot_of[...] + (q * SLOTS).astype(jnp.float32)
        for g in range(3):
            for v in range(SIDE):
                mix[g, :, v * TOK:(v + 1) * TOK] = jnp.transpose(jnp.where(
                    spread(v, ranks[g]) == slot, spread(v, weights[g]), 0.0)).astype(jnp.bfloat16)
        for h in (0, 1):
            for g, (first, width, axes) in enumerate(GROUPS):
                cols = half(g, h)
                came(back2[g].at[q, :, :, :, cols], r2_recv.at[g, q, h])
                total[g][:, cols] += dot(
                    mix[g], back2[g][q, :, :, :, cols].reshape(SIDE * TOK, cols.stop - cols.start))

                @pl.when(q == ROUNDS - 1)
                def _():
                    if h == 0:
                        went(blocks[g].at[pl.ds(0, 3 * TOK)], s1_send.at[g])
                    blocks[g][:, cols] = total[g][:, cols].astype(jnp.bfloat16)
                    far(g, h).start()
                    home(g, h, h == 1).start()
                    if h == 1:
                        leave(g).start()

    def along_x():
        came(pieces.at[mine, pl.ds(0, 7)], t_recv.at[0])
        for i in (2, 1, 3):
            su(i).start()

    def across():
        came(pieces.at[pl.ds(0, 3)], u_recv.at[1])
        sv().start()

    def shares():
        came(pieces.at[pl.ds(0, 4)], u_recv.at[0])
        for r in range(8):
            for p in range(8):
                table[r * 256 + p * PIECE:r * 256 + (p + 1) * PIECE, :] = pieces[p, r]
        logits = dot(normed[...], table[...])
        eye = jnp.where(iota((TOK, TOK), 0) == iota((TOK, TOK), 1), 1.0, 0.0).astype(jnp.bfloat16)
        member = dot_nt(eye, members().astype(jnp.bfloat16))
        powers = jnp.where(member > 0.5, jnp.exp(logits), 0.0)
        share = (powers / jnp.sum(powers, axis=1, keepdims=True)).astype(jnp.bfloat16)
        for g, (first, width, axes) in enumerate(GROUPS):
            shares_out[g] = dot_nt(holder(g), share).astype(jnp.bfloat16)
            weights[g, :, own(g)] = shares_out[g, pl.ds(pl.multiple_of(at[axes[0]] * 32, 32), 32), :]
        for g in range(3):
            for i in (2, 1, 3):
                sp(g, i).start()

    def prepare():
        came(weights.at[:, :, pl.ds(0, 3 * TOK)], p_recv.at[0])
        for g in range(3):
            total[g][...] = jnp.zeros(total[g].shape, jnp.float32)

    came(ranks.at[:, :, pl.ds(0, 3 * TOK)], q_recv.at[0])
    choose(0)
    for h in (0, 1):
        came(stacked.at[pl.ds(0, 3 * TOK), slice(0, 3 * HALF) if h == 0 else slice(3 * HALF, WIDTH)], s1_recv.at[h])
        gather(0, h)

    def step(k, carry):
        def stage(lag, run):
            @pl.when(jnp.logical_and(k >= lag, k < lag + ROUNDS))
            def _():
                run(k - lag)

        def once(when, run):
            @pl.when(k == when)
            def _():
                run()

        stage(0, whole_gather)
        once(0, along_x)
        once(1, across)
        stage(1, forward)
        once(2, shares)

        @pl.when(k == 2)
        def _():
            for load in loads:
                load.wait()

        stage(2, expert)
        once(3, prepare)
        stage(3, back)
        stage(5, combine)
        return carry

    lax.fori_loop(0, ROUNDS + 5, step, 0)

    for h in (0, 1):
        for g, (first, width, axes) in enumerate(GROUPS):
            cols = half(g, h)
            came(passing[g].at[:, cols], f_recv.at[g, h])
            rows = block(g, near(axes[0], 1 if h == 0 else 3))
            both = total[g][rows, cols] + passing[g][:, cols].astype(jnp.float32)
            blocks[g][rows, cols] = both.astype(jnp.bfloat16)
            home(g, h, h == 0).start()
    for g in range(3):
        came(blocks[g].at[pl.ds(0, 2 * TOK)], r1_recv.at[g])
    went(pieces.at[pl.ds(0, 4)], u_send.at[0])
    went(pieces.at[pl.ds(0, 3)], u_send.at[1])
    went(pieces.at[0, pl.ds(0, 7)], t_send.at[0])
    went(ranks.at[:, :, pl.ds(0, 3 * TOK)], q_send.at[0])
    went(weights.at[:, :, pl.ds(0, 3 * TOK)], p_send.at[0])
    for g in range(3):
        went(hop2[g].at[:, :, pl.ds(0, 7)], s3_send.at[g])
        went(hop2[g].at[:, :, pl.ds(0, 7)], r3_send.at[g])
        went(back3[g].at[:, pl.ds(0, 3)], r2_send.at[g])
        went(blocks[g].at[pl.ds(0, 3 * TOK)], r1_send.at[g])
        leave(g).wait()


def per_group(shape):
    return [pltpu.VMEM(shape(width), jnp.bfloat16) for _, width, _ in GROUPS]


def flat_kernel(*refs):
    args, rest = refs[:11], list(refs[11:])

    def take(n):
        head = rest[:n]
        del rest[:n]
        return head

    blocks = take(3)
    ranks, weights = take(2)
    packed, hop2, arrived, back3, back2, passing, total = (take(3) for _ in range(7))
    kernel(*args, blocks, ranks, weights, packed, hop2, arrived, back3, back2, passing, total, *rest)


def per_device(tokens, norm_gain, router, routes, placement, w_gate, w_up, w_down):
    dma = pltpu.SemaphoreType.DMA
    bf = jnp.bfloat16
    scratch = (
        per_group(lambda w: (SIDE * TOK, w))
        + [pltpu.VMEM((3, 32, SIDE * TOK), bf), pltpu.VMEM((3, 32, SIDE * TOK), bf)]
        + per_group(lambda w: (ROUNDS, 32, 16, w))
        + per_group(lambda w: (ROUNDS, 4, 8, 16, w))
        + per_group(lambda w: (ROUNDS, 8, 4, 16, w))
        + per_group(lambda w: (ROUNDS, 4, 8, 16, w))
        + per_group(lambda w: (ROUNDS, 4, 8, 16, w))
        + per_group(lambda w: (TOK, w))
        + [pltpu.VMEM((SIDE * TOK, w), jnp.float32) for _, w, _ in GROUPS]
        + [
            pltpu.VMEM((WIDTH, HIDDEN), bf),
            pltpu.VMEM((WIDTH, HIDDEN), bf),
            pltpu.VMEM((HIDDEN, WIDTH), bf),
            pltpu.VMEM((TOK, WIDTH), bf),
            pltpu.VMEM((WIDTH, DEVICES), bf),
            pltpu.VMEM((8, 8, PIECE, DEVICES), bf),
            pltpu.VMEM((SIDE * TOK, WIDTH), bf),
            pltpu.VMEM((SIDE * TOK, HIDDEN), bf),
            pltpu.VMEM((TOK, SIDE * TOK), jnp.float32),
            pltpu.VMEM((3, SIDE * TOK, SIDE * TOK), bf),
            pltpu.VMEM((TOK, WIDTH), bf),
            pltpu.VMEM((1, WIDTH), jnp.float32),
            pltpu.VMEM((8, TOK), jnp.int32),
            pltpu.VMEM((1, DEVICES), jnp.int32),
            pltpu.VMEM((3, DEVICES, TOK), bf),
            pltpu.VMEM((3, DEVICES, TOK), bf),
            dma((3,)), dma((5,)), dma((3,)),
            dma((1,)), dma((1,)),
            dma((2,)), dma((2,)),
            dma((3,)), dma((2,)),
            dma((1,)), dma((1,)),
            dma((1,)), dma((1,)),
            dma((ROUNDS,)), dma((3, ROUNDS)),
            dma((3,)), dma((ROUNDS,)),
            dma((3,)), dma((ROUNDS,)),
            dma((3,)), dma((3, ROUNDS, 2)),
            dma((3,)), dma((3,)), dma((3, 2)),
        ]
    )
    whole = pl.BlockSpec(memory_space=pl.ANY)
    own, low, high = pl.pallas_call(
        flat_kernel,
        name="moe",
        out_shape=[jax.ShapeDtypeStruct((TOK, WIDTH), bf)] * 3,
        in_specs=[whole] * 8,
        out_specs=[whole] * 3,
        scratch_shapes=scratch,
        compiler_params=pltpu.CompilerParams(
            collective_id=0, has_side_effects=True, vmem_limit_bytes=63 * 2**20
        ),
        cost_estimate=pl.CostEstimate(flops=15 * 10**9, bytes_accessed=11 * 10**6, transcendentals=10**6),
    )(tokens, norm_gain.reshape(1, WIDTH), router, routes.T, placement.reshape(1, DEVICES), w_gate, w_up, w_down)
    return (own.astype(jnp.float32) + low.astype(jnp.float32) + high.astype(jnp.float32)).astype(bf)


def solution(mesh):
    placed = (
        P(("rep", "expert"), None),
        P(),
        P("rep", None),
        P(("rep", "expert"), None),
        P(),
        P(("rep", "expert"), None, None),
        P(("rep", "expert"), None, None),
        P(("rep", "expert"), None, None),
    )
    return jax.shard_map(
        per_device,
        mesh=mesh,
        in_specs=placed,
        out_specs=P(("rep", "expert"), None),
        check_vma=False,
    )
```

```python
import jax
import jax.numpy as jnp
from jax import lax
from jax.experimental import pallas as pl
from jax.experimental.pallas import tpu as pltpu
from jax.sharding import PartitionSpec as P

MESH = pl.DeviceIdType.MESH
TOK = 128
WIDTH = 2048
HIDDEN = 768
SIDE = 4
ROUNDS = 3
SLOTS = 4
DEVICES = 128
GROUPS = (
    (0, 768, (2, 0, 1)),
    (768, 640, (0, 1, 2)),
    (1408, 640, (1, 2, 0)),
)
NT = (((1,), (1,)), ((), ()))
PIECE = 32
HALF = 384


def iota(shape, dim):
    return lax.broadcasted_iota(jnp.int32, shape, dim)


def dot(a, b):
    return jnp.dot(a, b, preferred_element_type=jnp.float32)


def dot_nt(a, b):
    return lax.dot_general(a, b, NT, preferred_element_type=jnp.float32)


def kernel(
    tokens, gain, router, routes, placement, w_gate, w_up, w_down, own_part, low_part, high_part,
    blocks, ranks, weights, packed, hop2, arrived, back3, back2, passing, total,
    gate_v, up_v, down_v, normed, table, pieces, stacked, hidden, slot_of, mix,
    tokens_v, gain_v, routes_v, placement_v, ranks_out, shares_out,
    w_sem, in_sem, out_sem, t_send, t_recv, u_send, u_recv,
    s1_send, s1_recv, q_send, q_recv, p_send, p_recv, s2_send, s2_recv, s3_send, s3_recv, r3_send, r3_recv, r2_send, r2_recv, r1_send, r1_recv, f_recv,
):
    rep = lax.axis_index("rep")
    exp = lax.axis_index("expert")
    core = exp % 2
    at = (rep // 2, (rep % 2) * 2 + exp // 8, (exp // 2) % 4)

    def device(pos, c):
        z, y, x = pos
        return (z * 2 + y // 2, (y % 2) * 8 + x * 2 + c)

    def along(axis, value, c):
        pos = list(at)
        pos[axis] = value
        return device(pos, c)

    def near(axis, step):
        return (at[axis] + step) % SIDE

    def remote(src, dst, send, recv, dev):
        return pltpu.make_async_remote_copy(
            src_ref=src, dst_ref=dst, send_sem=send, recv_sem=recv,
            device_id=dev, device_id_type=MESH,
        )

    def came(ref, sem):
        remote(ref, ref, sem, sem, device(at, 1 - core)).wait_recv()

    def went(ref, sem):
        remote(ref, ref, sem, sem, device(at, 1 - core)).wait_send()

    barrier = pltpu.get_barrier_semaphore()
    greeted = [along(a, near(a, i), (core + d) % 2) for a in range(3) for i in (1, 2, 3) for d in (0, 1)]
    greeted.append(device(at, 1 - core))
    greeted += [device((near(0, i), near(1, 2), at[2]), core) for i in (1, 2, 3)]
    for dev in greeted:
        pl.semaphore_signal(barrier, inc=1, device_id=dev, device_id_type=MESH)

    mine = core * 4 + at[2]
    operands = [
        pltpu.make_async_copy(tokens, tokens_v, in_sem.at[0]),
        pltpu.make_async_copy(gain, gain_v, in_sem.at[1]),
        pltpu.make_async_copy(routes, routes_v, in_sem.at[2]),
        pltpu.make_async_copy(placement, placement_v, in_sem.at[3]),
        pltpu.make_async_copy(
            router.at[pl.ds(pl.multiple_of(mine * PIECE, PIECE), PIECE)], pieces.at[mine, rep], in_sem.at[4]),
    ]
    for load in operands:
        load.start()
    loads = [
        pltpu.make_async_copy(w_gate.at[0], gate_v, w_sem.at[0]),
        pltpu.make_async_copy(w_up.at[0], up_v, w_sem.at[1]),
        pltpu.make_async_copy(w_down.at[0], down_v, w_sem.at[2]),
    ]
    for load in loads:
        load.start()

    operands[0].wait()
    operands[1].wait()
    values = tokens_v[...].astype(jnp.float32)
    scale = lax.rsqrt(jnp.mean(values * values, axis=-1, keepdims=True) + 1e-06)
    normed[...] = (values * scale * gain_v[...]).astype(jnp.bfloat16)
    for g, (first, width, axes) in enumerate(GROUPS):
        blocks[g][pl.ds(pl.multiple_of(at[axes[0]] * TOK, TOK), TOK), :] = normed[:, first:first + width]

    def holder(g):
        a1, a2, a3 = GROUPS[g][2]
        r = iota((DEVICES, DEVICES), 0)
        pos = [None, None, None]
        pos[a1] = r // 32
        pos[a2] = (r // 8) % 4
        pos[a3] = (r // 2) % 4
        wanted = pos[0] * 32 + pos[1] * 8 + pos[2] * 2 + r % 2
        return jnp.where(placement_v[...] == wanted, 1.0, 0.0).astype(jnp.bfloat16)

    def members():
        found = jnp.zeros((DEVICES, TOK), jnp.float32)
        rows = iota((DEVICES, TOK), 0)
        for k in range(8):
            found = found + jnp.where(routes_v[k:k + 1, :] == rows, 1.0, 0.0)
        return found

    operands[2].wait()
    operands[3].wait()
    member = members()
    before = jnp.where(iota((TOK, TOK), 0) < iota((TOK, TOK), 1), 1.0, 0.0).astype(jnp.bfloat16)
    rank = jnp.where(member > 0.5, dot(member.astype(jnp.bfloat16), before), -1.0).astype(jnp.bfloat16)
    for g, (first, width, axes) in enumerate(GROUPS):
        ranks_out[g] = dot(holder(g), rank).astype(jnp.bfloat16)
        ranks[g, :, pl.ds(pl.multiple_of(at[axes[0]] * TOK, TOK), TOK)] = ranks_out[
            g, pl.ds(pl.multiple_of(at[axes[0]] * 32, 32), 32), :]
    operands[4].wait()

    pl.semaphore_wait(barrier, len(greeted))

    def block(g, position):
        return pl.ds(pl.multiple_of(position * TOK, TOK), TOK)

    def own(g):
        return block(g, at[GROUPS[g][2][0]])

    def half(g, h):
        return slice(0, HALF) if h == 0 else slice(HALF, GROUPS[g][1])

    def s1(g, i, h):
        a = GROUPS[g][2][0]
        mine = blocks[g].at[own(g), half(g, h)]
        return remote(mine, mine, s1_send.at[g], s1_recv.at[h],
                      along(a, near(a, i), core))

    def sq(g, i):
        a = GROUPS[g][2][0]
        v = near(a, i)
        return remote(ranks_out.at[g, pl.ds(pl.multiple_of(v * 32, 32), 32)], ranks.at[g, :, own(g)],
                      q_send.at[0], q_recv.at[0], along(a, v, core))

    def sp(g, i):
        a = GROUPS[g][2][0]
        v = near(a, i)
        return remote(shares_out.at[g, pl.ds(pl.multiple_of(v * 32, 32), 32)], weights.at[g, :, own(g)],
                      p_send.at[0], p_recv.at[0], along(a, v, core))

    def st(i):
        return remote(pieces.at[mine, rep], pieces.at[mine, rep],
                      t_send.at[0], t_recv.at[0], ((rep + i) % 8, exp))

    def su(i):
        return remote(pieces.at[mine], pieces.at[mine],
                      u_send.at[1], u_recv.at[1], along(2, near(2, i), core))

    def sv():
        return remote(pieces.at[pl.ds(core * 4, 4)], pieces.at[pl.ds(core * 4, 4)],
                      u_send.at[0], u_recv.at[0], device(at, 1 - core))

    for i in (2, 1, 3):
        for g in range(3):
            s1(g, i, 0).start()
    for g in range(3):
        for i in (2, 1, 3):
            sq(g, i).start()
    for i in (2, 1, 3):
        for g in range(3):
            s1(g, i, 1).start()
    for i in range(1, 8):
        st(i).start()

    row = iota((TOK, SIDE * TOK), 0)
    col = iota((TOK, SIDE * TOK), 1)
    slot_of[...] = jnp.where((row // 4) % 4 == col // TOK, row % 4, 1000).astype(jnp.float32)

    def spread(v, plane):
        r = iota((TOK, 32), 0)
        pick = jnp.where(iota((TOK, 32), 1) == v * 8 + r // 16, 1.0, 0.0).astype(jnp.bfloat16)
        return dot(pick, plane)

    def swap(g):
        r = iota((256, 256), 0)
        c = iota((256, 256), 1)
        a, b, d, s = r // 64, (r // 16) % 4, (r // 4) % 4, r % 4
        if GROUPS[g][2][0] == 0:
            wanted = d * 64 + b * 16 + a * 4 + s
        else:
            wanted = a * 64 + d * 16 + b * 4 + s
        return jnp.where(c == wanted, 1.0, 0.0).astype(jnp.bfloat16)

    def s2(g, q, i, cols):
        a = GROUPS[g][2][1]
        v = near(a, i)
        return remote(packed[g].at[q, pl.ds(v * 8, 8), :, cols], hop2[g].at[q, at[a], :, :, cols],
                      s2_send.at[q], s2_recv.at[g, q], along(a, v, core))

    def s3(g, q, i, d):
        a = GROUPS[g][2][2]
        u, c = near(a, i), (core + d) % 2
        src = hop2[g].at[q, :, u * 2 + c]
        dst = arrived[g].at[q, core * 4 + at[a]]
        if i == 0 and d == 0:
            return pltpu.make_async_copy(src, dst, s3_recv.at[q])
        return remote(src, dst, s3_send.at[g], s3_recv.at[q], along(a, u, c))

    def r3(g, q, i, d):
        a = GROUPS[g][2][2]
        u, c = near(a, i), (core + d) % 2
        src = packed[g].at[q, pl.ds((c * 4 + u) * 4, 4)]
        dst = back3[g].at[q, :, at[a] * 2 + core]
        if i == 0 and d == 0:
            return pltpu.make_async_copy(src, dst, r3_recv.at[q])
        return remote(src, dst, r3_send.at[g], r3_recv.at[q], along(a, u, c))

    def r2(g, q, i, h):
        a = GROUPS[g][2][1]
        v = near(a, i)
        cols = half(g, h)
        src, dst = back3[g].at[q, v, :, :, cols], back2[g].at[q, at[a], :, :, cols]
        if i == 0:
            return pltpu.make_async_copy(src, dst, r2_recv.at[g, q, h])
        return remote(src, dst, r2_send.at[g], r2_recv.at[g, q, h], along(a, v, core))

    def far(g, h):
        a = GROUPS[g][2][0]
        cols = half(g, h)
        return remote(blocks[g].at[block(g, near(a, 2)), cols], passing[g].at[:, cols],
                      r1_send.at[g], f_recv.at[g, h], along(a, near(a, 1 if h == 0 else 3), core))

    def home(g, h, up):
        first, width, axes = GROUPS[g]
        a = axes[0]
        cols = half(g, h)
        v = near(a, 1 if up else 3)
        part = low_part if up else high_part
        return remote(blocks[g].at[block(g, v), cols], part.at[:, first + cols.start:first + cols.stop],
                      r1_send.at[g], r1_recv.at[g], along(a, v, core))

    PAIRS = [(i, d) for i in (2, 1, 3, 0) for d in (0, 1)]

    def choose(q):
        slot = slot_of[...] + jnp.asarray(q * SLOTS, jnp.float32)
        for i in range(SIDE):
            for g, (first, width, axes) in enumerate(GROUPS):
                mix[g, i * TOK:(i + 1) * TOK, :] = jnp.where(
                    spread(near(axes[1], i), ranks[g]) == slot, 1.0, 0.0).astype(jnp.bfloat16)

    def gather(q, h):
        for g, (first, width, axes) in enumerate(GROUPS):
            cols = slice(0, width) if h is None else half(g, h)
            rows = dot(mix[g], blocks[g][:, cols]).astype(jnp.bfloat16)
            rows = rows.reshape(SIDE, 8, 16, cols.stop - cols.start)
            for i in (2, 1, 3, 0):
                v = near(axes[1], i)
                if i == 0:
                    hop2[g][q, v, :, :, cols] = rows[i]
                else:
                    packed[g][q, pl.ds(v * 8, 8), :, cols] = rows[i]
                    s2(g, q, i, cols).start()

    def whole_gather(q):
        @pl.when(q > 0)
        def _():
            choose(q)
            gather(q, None)

    def forward(q):
        for g in range(3):
            came(hop2[g].at[q, pl.ds(0, 3)], s2_recv.at[g, q])
            for i, d in PAIRS:
                s3(g, q, i, d).start()

    def expert(q):
        for g, (first, width, axes) in enumerate(GROUPS):
            if g == 0:
                came(stacked, s3_recv.at[q])
            for c in (0, 1):
                part = arrived[g][q, pl.ds(c * 4, 4)]
                if axes[0] == 2:
                    for y in range(4):
                        for z in range(4):
                            at_row = c * 256 + z * 64 + y * 16
                            stacked[at_row:at_row + 16, first:first + width] = part[y, z]
                else:
                    stacked[c * 256:(c + 1) * 256, first:first + width] = dot(
                        swap(g), part.reshape(256, width)).astype(jnp.bfloat16)

        def tile(n, carry):
            cols = pl.ds(pl.multiple_of(n * 256, 256), 256)
            gate = dot(stacked[...], gate_v[:, cols])
            up = dot(stacked[...], up_v[:, cols])
            hidden[:, cols] = (gate / (1.0 + jnp.exp(-gate)) * up).astype(jnp.bfloat16)
            return carry

        lax.fori_loop(0, HIDDEN // 256, tile, 0)
        for g, (first, width, axes) in enumerate(GROUPS):
            result = dot(hidden[...], down_v[:, first:first + width]).astype(jnp.bfloat16)
            if g == 0:
                went(stacked.at[pl.ds(0, 3 * TOK)], s2_send.at[q])
            for c in (0, 1):
                half = result[c * 256:(c + 1) * 256]
                if axes[0] == 2:
                    half = half.reshape(4, 4, 16, width)
                    for y in range(4):
                        for z in range(4):
                            packed[g][q, c * 16 + y * 4 + z] = half[z, y]
                else:
                    packed[g][q, pl.ds(c * 16, 16)] = dot(swap(g), half).astype(jnp.bfloat16).reshape(16, 16, width)
            for i, d in PAIRS:
                r3(g, q, i, d).start()

    def back(q):
        came(stacked, r3_recv.at[q])
        for h in (0, 1):
            for i in (2, 1, 3, 0):
                for g in range(3):
                    r2(g, q, i, h).start()

    def leave(g):
        first, width, axes = GROUPS[g]
        return pltpu.make_async_copy(
            blocks[g].at[own(g)], own_part.at[:, first:first + width], out_sem.at[g])

    def combine(q):
        slot = slot_of[...] + (q * SLOTS).astype(jnp.float32)
        for g in range(3):
            for v in range(SIDE):
                mix[g, :, v * TOK:(v + 1) * TOK] = jnp.transpose(jnp.where(
                    spread(v, ranks[g]) == slot, spread(v, weights[g]), 0.0)).astype(jnp.bfloat16)
        for h in (0, 1):
            for g, (first, width, axes) in enumerate(GROUPS):
                cols = half(g, h)
                came(back2[g].at[q, :, :, :, cols], r2_recv.at[g, q, h])
                total[g][:, cols] += dot(
                    mix[g], back2[g][q, :, :, :, cols].reshape(SIDE * TOK, cols.stop - cols.start))

                @pl.when(q == ROUNDS - 1)
                def _():
                    if h == 0:
                        went(blocks[g].at[pl.ds(0, 3 * TOK)], s1_send.at[g])
                    blocks[g][:, cols] = total[g][:, cols].astype(jnp.bfloat16)
                    far(g, h).start()
                    home(g, h, h == 1).start()
                    if h == 1:
                        leave(g).start()

    def along_x():
        came(pieces.at[mine, pl.ds(0, 7)], t_recv.at[0])
        for i in (2, 1, 3):
            su(i).start()

    def across():
        came(pieces.at[pl.ds(0, 3)], u_recv.at[1])
        sv().start()

    def shares():
        came(pieces.at[pl.ds(0, 4)], u_recv.at[0])
        for r in range(8):
            for p in range(8):
                table[r * 256 + p * PIECE:r * 256 + (p + 1) * PIECE, :] = pieces[p, r]
        logits = dot(normed[...], table[...])
        eye = jnp.where(iota((TOK, TOK), 0) == iota((TOK, TOK), 1), 1.0, 0.0).astype(jnp.bfloat16)
        member = dot_nt(eye, members().astype(jnp.bfloat16))
        powers = jnp.where(member > 0.5, jnp.exp(logits), 0.0)
        share = (powers / jnp.sum(powers, axis=1, keepdims=True)).astype(jnp.bfloat16)
        for g, (first, width, axes) in enumerate(GROUPS):
            shares_out[g] = dot_nt(holder(g), share).astype(jnp.bfloat16)
            weights[g, :, own(g)] = shares_out[g, pl.ds(pl.multiple_of(at[axes[0]] * 32, 32), 32), :]
        for g in range(3):
            for i in (2, 1, 3):
                sp(g, i).start()

    def prepare():
        came(weights.at[:, :, pl.ds(0, 3 * TOK)], p_recv.at[0])
        for g in range(3):
            total[g][...] = jnp.zeros(total[g].shape, jnp.float32)

    came(ranks.at[:, :, pl.ds(0, 3 * TOK)], q_recv.at[0])
    choose(0)
    for h in (0, 1):
        came(stacked.at[pl.ds(0, 3 * TOK), slice(0, 3 * HALF) if h == 0 else slice(3 * HALF, WIDTH)], s1_recv.at[h])
        gather(0, h)

    def step(k, carry):
        def stage(lag, run):
            @pl.when(jnp.logical_and(k >= lag, k < lag + ROUNDS))
            def _():
                run(k - lag)

        def once(when, run):
            @pl.when(k == when)
            def _():
                run()

        stage(0, whole_gather)
        once(0, along_x)
        once(1, across)
        stage(1, forward)
        once(2, shares)

        @pl.when(k == 2)
        def _():
            for load in loads:
                load.wait()

        stage(2, expert)
        once(3, prepare)
        stage(3, back)
        stage(5, combine)
        return carry

    lax.fori_loop(0, ROUNDS + 5, step, 0)

    for h in (0, 1):
        for g, (first, width, axes) in enumerate(GROUPS):
            cols = half(g, h)
            came(passing[g].at[:, cols], f_recv.at[g, h])
            rows = block(g, near(axes[0], 1 if h == 0 else 3))
            both = total[g][rows, cols] + passing[g][:, cols].astype(jnp.float32)
            blocks[g][rows, cols] = both.astype(jnp.bfloat16)
            home(g, h, h == 0).start()
    for g in range(3):
        came(blocks[g].at[pl.ds(0, 2 * TOK)], r1_recv.at[g])
    went(pieces.at[pl.ds(0, 4)], u_send.at[0])
    went(pieces.at[pl.ds(0, 3)], u_send.at[1])
    went(pieces.at[0, pl.ds(0, 7)], t_send.at[0])
    went(ranks.at[:, :, pl.ds(0, 3 * TOK)], q_send.at[0])
    went(weights.at[:, :, pl.ds(0, 3 * TOK)], p_send.at[0])
    for g in range(3):
        went(hop2[g].at[:, :, pl.ds(0, 7)], s3_send.at[g])
        went(hop2[g].at[:, :, pl.ds(0, 7)], r3_send.at[g])
        went(back3[g].at[:, pl.ds(0, 3)], r2_send.at[g])
        went(blocks[g].at[pl.ds(0, 3 * TOK)], r1_send.at[g])
        leave(g).wait()


def per_group(shape):
    return [pltpu.VMEM(shape(width), jnp.bfloat16) for _, width, _ in GROUPS]


def flat_kernel(*refs):
    args, rest = refs[:11], list(refs[11:])

    def take(n):
        head = rest[:n]
        del rest[:n]
        return head

    blocks = take(3)
    ranks, weights = take(2)
    packed, hop2, arrived, back3, back2, passing, total = (take(3) for _ in range(7))
    kernel(*args, blocks, ranks, weights, packed, hop2, arrived, back3, back2, passing, total, *rest)


def per_device(tokens, norm_gain, router, routes, placement, w_gate, w_up, w_down):
    dma = pltpu.SemaphoreType.DMA
    bf = jnp.bfloat16
    scratch = (
        per_group(lambda w: (SIDE * TOK, w))
        + [pltpu.VMEM((3, 32, SIDE * TOK), bf), pltpu.VMEM((3, 32, SIDE * TOK), bf)]
        + per_group(lambda w: (ROUNDS, 32, 16, w))
        + per_group(lambda w: (ROUNDS, 4, 8, 16, w))
        + per_group(lambda w: (ROUNDS, 8, 4, 16, w))
        + per_group(lambda w: (ROUNDS, 4, 8, 16, w))
        + per_group(lambda w: (ROUNDS, 4, 8, 16, w))
        + per_group(lambda w: (TOK, w))
        + [pltpu.VMEM((SIDE * TOK, w), jnp.float32) for _, w, _ in GROUPS]
        + [
            pltpu.VMEM((WIDTH, HIDDEN), bf),
            pltpu.VMEM((WIDTH, HIDDEN), bf),
            pltpu.VMEM((HIDDEN, WIDTH), bf),
            pltpu.VMEM((TOK, WIDTH), bf),
            pltpu.VMEM((WIDTH, DEVICES), bf),
            pltpu.VMEM((8, 8, PIECE, DEVICES), bf),
            pltpu.VMEM((SIDE * TOK, WIDTH), bf),
            pltpu.VMEM((SIDE * TOK, HIDDEN), bf),
            pltpu.VMEM((TOK, SIDE * TOK), jnp.float32),
            pltpu.VMEM((3, SIDE * TOK, SIDE * TOK), bf),
            pltpu.VMEM((TOK, WIDTH), bf),
            pltpu.VMEM((1, WIDTH), jnp.float32),
            pltpu.VMEM((8, TOK), jnp.int32),
            pltpu.VMEM((1, DEVICES), jnp.int32),
            pltpu.VMEM((3, DEVICES, TOK), bf),
            pltpu.VMEM((3, DEVICES, TOK), bf),
            dma((3,)), dma((5,)), dma((3,)),
            dma((1,)), dma((1,)),
            dma((2,)), dma((2,)),
            dma((3,)), dma((2,)),
            dma((1,)), dma((1,)),
            dma((1,)), dma((1,)),
            dma((ROUNDS,)), dma((3, ROUNDS)),
            dma((3,)), dma((ROUNDS,)),
            dma((3,)), dma((ROUNDS,)),
            dma((3,)), dma((3, ROUNDS, 2)),
            dma((3,)), dma((3,)), dma((3, 2)),
        ]
    )
    whole = pl.BlockSpec(memory_space=pl.ANY)
    own, low, high = pl.pallas_call(
        flat_kernel,
        name="moe",
        out_shape=[jax.ShapeDtypeStruct((TOK, WIDTH), bf)] * 3,
        in_specs=[whole] * 8,
        out_specs=[whole] * 3,
        scratch_shapes=scratch,
        compiler_params=pltpu.CompilerParams(
            collective_id=0, has_side_effects=True, vmem_limit_bytes=63 * 2**20
        ),
        cost_estimate=pl.CostEstimate(flops=15 * 10**9, bytes_accessed=11 * 10**6, transcendentals=10**6),
    )(tokens, norm_gain.reshape(1, WIDTH), router, routes.T, placement.reshape(1, DEVICES), w_gate, w_up, w_down)
    return (own.astype(jnp.float32) + low.astype(jnp.float32) + high.astype(jnp.float32)).astype(bf)


def solution(mesh):
    placed = (
        P(("rep", "expert"), None),
        P(),
        P("rep", None),
        P(("rep", "expert"), None),
        P(),
        P(("rep", "expert"), None, None),
        P(("rep", "expert"), None, None),
        P(("rep", "expert"), None, None),
    )
    return jax.shard_map(
        per_device,
        mesh=mesh,
        in_specs=placed,
        out_specs=P(("rep", "expert"), None),
        check_vma=False,
    )
```
